32 devices in a mesh: row: 2 (over core), col: 8 (over z, y), layer: 2 (over x).
Axes of the slice: x: 2, y: 2, z: 4, core: 2. Of those that a mesh axis runs over, the one named last changes fastest.
Arguments:
- flow_cols: int32 [16, 2, 8], P('row', 'layer', 'col'), may hold values from 0 to 64, as said below
- flow_vals: bfloat16 [16, 2, 8, 128, 128], P('row', 'layer', 'col'), may hold values from -22 to 22
- window_flow: bfloat16 [2, 8192, 4096], P('layer', 'row', 'col'), may hold values from -0.396875 to 0.396875
Outputs:
- flow_next: float32 [2048, 4096], P(('row', 'layer'), 'col')
The draws below stay inside these ranges and needn't reach their ends.
Inputs may be any that keep to these rules, and one draw needn't show every extreme that they name: `flow_cols`: an entry 64 marks an empty slot; the live entries of one block row and layer are distinct; every block row and layer has at least one live slot, and some block row and layer has all 8 slots live.
All inputs are finite; a program needn't handle non-finite values.
Results may differ from the reference program's by a relative error of at most 0.0003.
Values may be sent and summed in bfloat16 or wider, within the bound.
No kernel may reach another device: no remote copies, remote signals or barrier semaphores. Data moves between devices by JAX's collectives and lax.ppermute only.
A program may use at most 128 MiB of HBM per device.

```python
import math
import jax
import jax.numpy as jnp
from jax import lax

BS = 128
KL = 64
NR = 16
NW = 32
SL = 8
N_LAYER = 2


def draw_flow_cols(key, part):
    scores = jax.random.randint(jax.random.fold_in(key, 11), (NR, N_LAYER, KL), 0, 1 << 20)
    ordering = jnp.argsort(scores * KL + jnp.arange(KL, dtype=jnp.int32), axis=-1, stable=True)
    chosen = ordering[:, :, :SL].astype(jnp.int32)
    counts = jax.random.randint(jax.random.fold_in(key, 12), (NR, N_LAYER, 1), 1, SL + 1)
    full_row = jax.random.randint(jax.random.fold_in(key, 13), (), 0, NR * N_LAYER)
    flat_index = jnp.arange(NR, dtype=jnp.int32)[:, None] * N_LAYER + jnp.arange(N_LAYER, dtype=jnp.int32)[None, :]
    counts = jnp.where(flat_index[:, :, None] == full_row, SL, counts)
    slot_scores = jax.random.randint(jax.random.fold_in(key, 14), (NR, N_LAYER, SL), 0, 1 << 20)
    slot_order = jnp.argsort(slot_scores * SL + jnp.arange(SL, dtype=jnp.int32), axis=-1, stable=True)
    slot_rank = jnp.argsort(slot_order, axis=-1, stable=True)
    return jnp.where(slot_rank < counts, chosen, KL).astype(jnp.int32)


def draw_flow_vals(key, part):
    shape = (NR, N_LAYER, SL, BS, BS)
    row_ramp = jnp.arange(NR * BS, dtype=jnp.float32) / max(NR * BS - 1, 1)
    spread = jax.random.uniform(jax.random.fold_in(key, 22), (NR * BS,), jnp.float32, 0.0, 1.0)
    base_draw = jnp.clip(jax.random.normal(jax.random.fold_in(key, 21), shape, jnp.float32), -4.0, 4.0)
    row_scale = jnp.exp(0.5 * math.log(3.0) * row_ramp + 0.5 * math.log(10.0) * spread)
    row_scale = row_scale.reshape(NR, 1, 1, BS, 1)
    return (base_draw * row_scale).astype(jnp.bfloat16)


def draw_window_flow(key, part):
    shape = (N_LAYER, KL * BS, NW * BS)
    weight_scale = 1.0 / math.sqrt(N_LAYER * SL * BS // 2)
    column_scale = jnp.exp(0.5 * math.log(10.0) * jax.random.uniform(jax.random.fold_in(key, 31), (NW * BS,), jnp.float32, 0.0, 1.0))
    base_draw = jnp.clip(jax.random.normal(jax.random.fold_in(key, 33), shape, jnp.float32), -4.0, 4.0)
    return (base_draw * column_scale[None, None, :] * weight_scale).astype(jnp.bfloat16)


def setup_inputs(seed: int = 0) -> dict:
    seeds = jax.random.split(jax.random.key(seed), 4)
    flow_cols = draw_flow_cols(jax.random.fold_in(seeds[3], 71), 0)
    flow_vals = draw_flow_vals(jax.random.fold_in(seeds[3], 71), 0)
    window_flow = draw_window_flow(jax.random.fold_in(seeds[3], 71), 0)
    return dict(flow_cols=flow_cols, flow_vals=flow_vals, window_flow=window_flow)


def reference(flow_cols, flow_vals, window_flow):
    window_blocks = window_flow.reshape(N_LAYER, KL, BS, NW * BS)

    def one_row(row_data):
        row_cols, row_vals = row_data

        def one_layer(running, layer_data):
            layer_blocks, layer_cols, layer_vals = layer_data
            slot_live = layer_cols < KL
            picked = jnp.take(layer_blocks, jnp.minimum(layer_cols, KL - 1).astype(jnp.int32), axis=0)
            masked = jnp.where(slot_live[:, None, None], layer_vals, jnp.zeros_like(layer_vals))
            product = jnp.einsum('sab,sbc->ac', masked.astype(jnp.float32), picked.astype(jnp.float32))
            return running + product, None

        start_value = jnp.zeros((BS, NW * BS), jnp.float32)
        running, unused = lax.scan(one_layer, start_value, (window_blocks, row_cols, row_vals))
        return running

    expanded = lax.map(one_row, (flow_cols, flow_vals)).reshape(NR * BS, NW * BS)
    squares = expanded * expanded
    column_mean = jnp.mean(squares, axis=0)
    return squares / (column_mean + 1e-6)
```

```python
import functools

import jax
import jax.numpy as jnp
from jax import lax
from jax.experimental import pallas as pl
from jax.experimental.pallas import tpu as pltpu
from jax.sharding import PartitionSpec as P

CODE_SPAN = 250.0
CODE_MID = 125.0
LOG2E = 1.4426950408889634
ID_ROWS = 16
VMEM_BYTES = 48 * 1024 * 1024


def pack_kernel(cols_ref, layer_ref, vals_ref, send_ref, keep_ref, ids, sems):
    rows = send_ref.shape[0] - ID_ROWS
    block = vals_ref.shape[1]
    count = rows // block
    layer = layer_ref[0]
    copies = []
    for k, (out, part) in enumerate(((send_ref, 1 - layer), (keep_ref, layer))):
        copies.append(
            pltpu.make_async_copy(
                vals_ref.at[pl.ds(pl.multiple_of(part * rows, block), rows)],
                out.at[pl.ds(0, rows)],
                sems.at[2 * k],
            )
        )
        copies[-1].start()
        lanes = lax.broadcasted_iota(jnp.int32, (ID_ROWS, block), 1)
        line = jnp.zeros((ID_ROWS, block), jnp.int32)
        for j in range(count):
            line = jnp.where(lanes == j, cols_ref[part * count + j, 0, 0], line)
        ids[k] = line.astype(jnp.float32).astype(jnp.bfloat16)
        copies.append(
            pltpu.make_async_copy(ids.at[k], out.at[pl.ds(rows, ID_ROWS)], sems.at[2 * k + 1])
        )
        copies[-1].start()
    for copy in copies:
        copy.wait()


def products(items, row, own, other, flat, blocks, ids_v, ids_s, sem_id, sem_a, sem_b, finish):
    block = flat.shape[1] // len(items)
    rows = flat.shape[0]
    count = rows // block
    slots = len(items)
    half = own.shape[0] // block
    for s, item in enumerate(items):
        ids_v[pl.ds(s, 1)] = item[rows : rows + 1, :].astype(jnp.float32).astype(jnp.int32)
    to_scalar = pltpu.make_async_copy(ids_v, ids_s, sem_id)
    to_scalar.start()
    for s, item in enumerate(items):
        flat[:, s * block : (s + 1) * block] = item[0:rows, :]
    to_scalar.wait()
    depth = blocks.shape[0]

    def fetch(j):
        for s in range(slots):
            col = jnp.minimum(ids_s[s, j], 2 * half - 1)
            local = lax.rem(col, half)
            here = lax.div(col, half) == row
            where = pl.ds(pl.multiple_of(local * block, block), block)
            target = blocks.at[j % depth, pl.ds(s * block, block)]

            @pl.when(here)
            def _():
                pltpu.make_async_copy(own.at[where], target, sem_b.at[j % depth]).start()

            @pl.when(jnp.logical_not(here))
            def _():
                pltpu.make_async_copy(other.at[where], target, sem_b.at[j % depth]).start()

    for j in range(min(depth, count)):
        fetch(j)
    for j in range(count):
        pieces = []
        for s in range(slots):
            live = jnp.where(ids_s[s, j] < 2 * half, 1.0, 0.0).astype(jnp.float32)
            piece = flat[j * block : (j + 1) * block, s * block : (s + 1) * block]
            pieces.append((piece.astype(jnp.float32) * live).astype(jnp.bfloat16))
        whole = blocks.at[j % depth]
        pltpu.make_async_copy(whole, whole, sem_b.at[j % depth]).wait()
        left = jnp.concatenate(pieces, axis=1)
        finish(j, jnp.dot(left, blocks[j % depth], preferred_element_type=jnp.float32))
        if j + depth < count:
            fetch(j + depth)


def send_kernel(slots, row_ref, *refs):
    items, (own, other, code_ref, flat, blocks, ids_v, ids_s, total, sem_id, sem_b) = refs[:slots], refs[slots:]
    block = flat.shape[1] // slots
    rows = flat.shape[0]

    def finish(j, value):
        total[j * block : (j + 1) * block, :] = value

    products(items, row_ref[0], own, other, flat, blocks, ids_v, ids_s, sem_id, None, sem_b, finish)
    most = jnp.max(jnp.abs(total[...]), axis=0, keepdims=True)
    scale = (most * 1.01 + 1e-30).astype(jnp.bfloat16)
    inverse = CODE_SPAN / scale.astype(jnp.float32)
    for j in range(rows // block):
        value = total[j * block : (j + 1) * block, :]
        size = jnp.exp((jnp.abs(value) * inverse - CODE_MID) * (1.0 / LOG2E))
        code_ref[j * block : (j + 1) * block, :] = jnp.where(value < 0, -size, size).astype(jnp.bfloat16)
    code_ref[rows : rows + ID_ROWS, :] = jnp.broadcast_to(scale, (ID_ROWS, scale.shape[1]))


def keep_kernel(slots, row_ref, *refs):
    items, rest = refs[:slots], refs[slots:]
    own, other, code_ref, square_ref, sum_ref, flat, blocks, ids_v, ids_s, sem_id, sem_b = rest
    block = flat.shape[1] // slots
    rows = flat.shape[0]
    scale = code_ref[rows : rows + 1, :].astype(jnp.float32) * (1.0 / CODE_SPAN)
    sums = []

    def finish(j, value):
        code = code_ref[j * block : (j + 1) * block, :].astype(jnp.float32)
        size = (jnp.log(jnp.abs(code)) * LOG2E + CODE_MID) * scale
        full = value + jnp.where(code < 0, -size, size)
        square = full * full
        square_ref[j * block : (j + 1) * block, :] = square
        sums.append(jnp.sum(square, axis=0, keepdims=True))

    products(items, row_ref[0], own, other, flat, blocks, ids_v, ids_s, sem_id, None, sem_b, finish)
    sum_ref[...] = functools.reduce(jnp.add, sums)


def ring_of(mesh):
    size = mesh.shape["col"]
    if size != 8:
        return list(range(size))
    return [0, 2, 4, 6, 7, 5, 3, 1]


def solution(mesh):
    size = mesh.shape["col"]
    order = ring_of(mesh)
    ahead = [(order[i], order[(i + 1) % size]) for i in range(size)]
    back = [(b, a) for a, b in ahead]
    swap = [(0, 1), (1, 0)]
    vmem = pl.BlockSpec(memory_space=pltpu.VMEM)
    smem = pl.BlockSpec(memory_space=pltpu.SMEM)
    anywhere = pl.BlockSpec(memory_space=pl.ANY)

    def gather(item, last_ahead):
        items = [item]
        front = rear = item
        for step in range(1, size // 2 + 1):
            if step < size // 2 or last_ahead:
                front = lax.ppermute(front, "col", ahead)
                items.append(front)
            if step < size // 2 or not last_ahead:
                rear = lax.ppermute(rear, "col", back)
                items.append(rear)
        return items

    def gather_all(item):
        stacked = lax.all_gather(item, "col", axis=0)
        return [stacked[i] for i in range(size)]

    def body(flow_cols, flow_vals, window_flow):
        block = flow_vals.shape[-1]
        count = flow_vals.shape[0] // 2
        rows = count * block
        own = window_flow[0]
        columns = own.shape[1]
        other = lax.ppermute(own, "row", swap)
        row = lax.axis_index("row").astype(jnp.int32).reshape(1)
        layer = lax.axis_index("layer").astype(jnp.int32).reshape(1)
        item = jax.ShapeDtypeStruct((rows + ID_ROWS, block), flow_vals.dtype)
        send, keep = pl.pallas_call(
            pack_kernel,
            out_shape=(item, item),
            in_specs=[smem, smem, anywhere],
            out_specs=(anywhere, anywhere),
            scratch_shapes=[pltpu.VMEM((2, ID_ROWS, block), flow_vals.dtype), pltpu.SemaphoreType.DMA((4,))],
        )(flow_cols, layer, flow_vals.reshape(2 * rows, block))
        if size == 8:
            sends, keeps = gather(send, True), gather(keep, False)
        else:
            sends, keeps = gather_all(send), gather_all(keep)
        depth = count if size <= 8 else 1
        scratch = [
            pltpu.VMEM((rows, size * block), flow_vals.dtype),
            pltpu.VMEM((depth, size * block, columns), own.dtype),
            pltpu.VMEM((max(size, 8), block), jnp.int32),
            pltpu.SMEM((max(size, 8), block), jnp.int32),
        ]
        sems = [pltpu.SemaphoreType.DMA(()), pltpu.SemaphoreType.DMA((depth,))]
        params = pltpu.CompilerParams(vmem_limit_bytes=VMEM_BYTES)
        code = pl.pallas_call(
            functools.partial(send_kernel, size),
            out_shape=jax.ShapeDtypeStruct((rows + ID_ROWS, columns), jnp.bfloat16),
            in_specs=[smem] + [vmem] * size + [anywhere] * 2,
            out_specs=vmem,
            scratch_shapes=scratch + [pltpu.VMEM((rows, columns), jnp.float32)] + sems,
            compiler_params=params,
        )(row, *sends, own, other)
        code = lax.ppermute(code, "layer", swap)
        square, sums = pl.pallas_call(
            functools.partial(keep_kernel, size),
            out_shape=(
                jax.ShapeDtypeStruct((rows, columns), jnp.float32),
                jax.ShapeDtypeStruct((1, columns), jnp.float32),
            ),
            in_specs=[smem] + [vmem] * size + [anywhere] * 2 + [vmem],
            out_specs=(vmem, vmem),
            scratch_shapes=scratch + sems,
            compiler_params=params,
        )(row, *keeps, own, other, code)
        sums = sums + lax.ppermute(sums, "row", swap)
        sums = sums + lax.ppermute(sums, "layer", swap)
        total_rows = rows * lax.axis_size("row") * lax.axis_size("layer")
        return square * (1.0 / (sums / total_rows + 1e-6))

    placed = (
        P("row", "layer", "col"),
        P("row", "layer", "col", None, None),
        P("layer", "row", "col"),
    )
    return jax.shard_map(body, mesh=mesh, in_specs=placed, out_specs=P(("row", "layer"), "col"), check_vma=False)
```

```python
import functools

import jax
import jax.numpy as jnp
from jax import lax
from jax.experimental import pallas as pl
from jax.experimental.pallas import tpu as pltpu
from jax.sharding import PartitionSpec as P

CODE_SPAN = 250.0
CODE_MID = 125.0
LOG2E = 1.4426950408889634
ID_ROWS = 16
VMEM_BYTES = 24 * 1024 * 1024
AFTER = {5: 3}
JOIN_AT = (2, 3)
PLACE_LIMIT = 24 << 20


def pack_kernel(cols_ref, layer_ref, vals_ref, send_ref, keep_ref, sems):
    rows = send_ref.shape[0] - ID_ROWS
    block = vals_ref.shape[1]
    count = rows // block
    layer = layer_ref[0]
    copies = []
    for k, (out, part) in enumerate(((send_ref, 1 - layer), (keep_ref, layer))):
        copies.append(
            pltpu.make_async_copy(
                vals_ref.at[pl.ds(pl.multiple_of(part * rows, block), rows)],
                out.at[pl.ds(0, rows)],
                sems.at[k],
            )
        )
        copies[-1].start()
        lanes = lax.broadcasted_iota(jnp.int32, (ID_ROWS, block), 1)
        line = jnp.zeros((ID_ROWS, block), jnp.int32)
        for j in range(count):
            line = jnp.where(lanes == j, cols_ref[part * count + j], line)
        out[rows : rows + ID_ROWS, :] = line.astype(jnp.float32).astype(jnp.bfloat16)
    for copy in copies:
        copy.wait()


def place_kernel(at_ref, part_ref, *refs):
    window_ref, sem = refs[-2:]
    half = part_ref.shape[0]
    where = pl.ds(pl.multiple_of(at_ref[0] * half, half), half)
    copy = pltpu.make_async_copy(part_ref, window_ref.at[where], sem)
    copy.start()
    copy.wait()


def products(items, window, first, ids_v, ids_s, sems, finish):
    block = first.shape[1]
    rows = first.shape[0] - ID_ROWS
    live_end = window.shape[0] // block
    fetch = pltpu.make_async_copy(items[0], first, sems.at[0])
    fetch.start()
    for s in range(1, len(items)):
        ids_v[pl.ds(s, 1)] = items[s][rows : rows + 1, :].astype(jnp.float32).astype(jnp.int32)
    fetch.wait()
    ids_v[pl.ds(0, 1)] = first[rows : rows + 1, :].astype(jnp.float32).astype(jnp.int32)
    to_scalar = pltpu.make_async_copy(ids_v, ids_s, sems.at[1])
    to_scalar.start()
    to_scalar.wait()
    for j in range(rows // block):
        left, right = [], []
        for s in range(len(items)):
            col = ids_s[s, j]
            live = jnp.where(col < live_end, 1.0, 0.0).astype(jnp.float32)
            source = first if s == 0 else items[s]
            piece = source[j * block : (j + 1) * block, :]
            left.append((piece.astype(jnp.float32) * live).astype(jnp.bfloat16))
            at = pl.multiple_of(jnp.minimum(col, live_end - 1) * block, block)
            right.append(window[pl.ds(at, block), :])
        finish(
            j,
            jnp.dot(
                jnp.concatenate(left, axis=1),
                jnp.concatenate(right, axis=0),
                preferred_element_type=jnp.float32,
            ),
        )


def send_kernel(slots, *refs):
    items, (window, code_ref, first, ids_v, ids_s, total, sems) = refs[:slots], refs[slots:]
    block = first.shape[1]
    rows = total.shape[0]

    def finish(j, value):
        total[j * block : (j + 1) * block, :] = value

    products(items, window, first, ids_v, ids_s, sems, finish)
    most = jnp.max(jnp.abs(total[...]), axis=0, keepdims=True)
    scale = (most * 1.01 + 1e-30).astype(jnp.bfloat16)
    inverse = CODE_SPAN / scale.astype(jnp.float32)
    for j in range(rows // block):
        value = total[j * block : (j + 1) * block, :]
        size = jnp.exp((jnp.abs(value) * inverse - CODE_MID) * (1.0 / LOG2E))
        code_ref[j * block : (j + 1) * block, :] = jnp.where(value < 0, -size, size).astype(jnp.bfloat16)
    code_ref[rows : rows + ID_ROWS, :] = jnp.broadcast_to(scale, (ID_ROWS, scale.shape[1]))


def keep_kernel(slots, *refs):
    items, (window, code_ref, square_ref, sum_ref, first, ids_v, ids_s, sems) = refs[:slots], refs[slots:]
    block = first.shape[1]
    rows = square_ref.shape[0]
    scale = code_ref[rows : rows + 1, :].astype(jnp.float32) * (1.0 / CODE_SPAN)
    sums = []

    def finish(j, value):
        code = code_ref[j * block : (j + 1) * block, :].astype(jnp.float32)
        size = (jnp.log(jnp.abs(code)) * LOG2E + CODE_MID) * scale
        full = value + jnp.where(code < 0, -size, size)
        square = full * full
        square_ref[j * block : (j + 1) * block, :] = square
        sums.append(jnp.sum(square, axis=0, keepdims=True))

    products(items, window, first, ids_v, ids_s, sems, finish)
    sum_ref[...] = functools.reduce(jnp.add, sums)


def ring_of(mesh):
    size = mesh.shape["col"]
    if size != 8:
        return list(range(size))
    return [0, 2, 4, 6, 7, 5, 3, 1]


def solution(mesh):
    size = mesh.shape["col"]
    order = ring_of(mesh)
    ahead = [(order[i], order[(i + 1) % size]) for i in range(size)]
    back = [(b, a) for a, b in ahead]
    swap = [(0, 1), (1, 0)]
    vmem = pl.BlockSpec(memory_space=pltpu.VMEM)
    smem = pl.BlockSpec(memory_space=pltpu.SMEM)
    anywhere = pl.BlockSpec(memory_space=pl.ANY)

    def step_on(ends, items, forward=True, backward=True):
        front, rear = ends
        if forward:
            front = lax.ppermute(front, "col", ahead)
            items.append(front)
        if backward:
            rear = lax.ppermute(rear, "col", back)
            items.append(rear)
        return front, rear

    def gather_two(send, keep, window, join):
        sends, keeps = [send], [keep]
        at, behind = (send, send), (keep, keep)
        last = size // 2
        done = 0
        for step in range(1, last + 2):
            want = AFTER.get(step, 0)
            while done < want:
                done += 1
                behind = step_on(behind, keeps, done < last, True)
            if want:
                at, behind = lax.optimization_barrier((at, behind))
            if step == JOIN_AT[1]:
                window = join(window)
            if step in JOIN_AT:
                at, window = lax.optimization_barrier((at, window))
            if step <= last:
                at = step_on(at, sends, True, step < last)
        sends[-1] = at[0]
        while done < last:
            done += 1
            behind = step_on(behind, keeps, done < last, True)
        return sends, keeps, window

    def gather_all(item):
        stacked = lax.all_gather(item, "col", axis=0)
        return [stacked[i] for i in range(size)]

    def body(flow_cols, flow_vals, window_flow):
        block = flow_vals.shape[-1]
        count = flow_vals.shape[0] // 2
        rows = count * block
        own = window_flow[0]
        half, columns = own.shape
        other = lax.ppermute(own, "row", swap)
        row = lax.axis_index("row").astype(jnp.int32).reshape(1)
        layer = lax.axis_index("layer").astype(jnp.int32).reshape(1)
        item = jax.ShapeDtypeStruct((rows + ID_ROWS, block), flow_vals.dtype)
        params = pltpu.CompilerParams(vmem_limit_bytes=VMEM_BYTES)
        send, keep = pl.pallas_call(
            pack_kernel,
            out_shape=(item, item),
            in_specs=[smem, smem, anywhere],
            out_specs=(vmem, vmem),
            scratch_shapes=[pltpu.SemaphoreType.DMA((2,))],
        )(flow_cols.reshape(2 * count), layer, flow_vals.reshape(2 * rows, block))
        def place(at, part, window=None):
            given = [] if window is None else [window]
            return pl.pallas_call(
                place_kernel,
                out_shape=jax.ShapeDtypeStruct((2 * half, columns), own.dtype),
                in_specs=[smem, anywhere] + [vmem] * len(given),
                out_specs=vmem,
                scratch_shapes=[pltpu.SemaphoreType.DMA(())],
                input_output_aliases={2: 0} if given else {},
                compiler_params=pltpu.CompilerParams(vmem_limit_bytes=PLACE_LIMIT),
                cost_estimate=pl.CostEstimate(flops=0, bytes_accessed=2 * half * columns * 2, transcendentals=0),
            )(at, part, *given)

        window = place(row, own)
        if size == 8:
            sends, keeps, window = gather_two(send, keep, window, lambda w: place(1 - row, other, w))
        else:
            sends, keeps = gather_all(send), gather_all(keep)
            window = place(1 - row, other, window)
        scratch = [
            pltpu.VMEM((rows + ID_ROWS, block), flow_vals.dtype),
            pltpu.VMEM((max(size, 8), block), jnp.int32),
            pltpu.SMEM((max(size, 8), block), jnp.int32),
        ]
        sems = [pltpu.SemaphoreType.DMA((2,))]
        item_specs = [anywhere] + [vmem] * (size - 1)
        code = pl.pallas_call(
            functools.partial(send_kernel, size),
            out_shape=jax.ShapeDtypeStruct((rows + ID_ROWS, columns), jnp.bfloat16),
            in_specs=item_specs + [vmem],
            out_specs=vmem,
            scratch_shapes=scratch + [pltpu.VMEM((rows, columns), jnp.float32)] + sems,
            compiler_params=params,
        )(*sends, window)
        code = lax.ppermute(code, "layer", swap)
        square, sums = pl.pallas_call(
            functools.partial(keep_kernel, size),
            out_shape=(
                jax.ShapeDtypeStruct((rows, columns), jnp.float32),
                jax.ShapeDtypeStruct((1, columns), jnp.float32),
            ),
            in_specs=item_specs + [vmem, vmem],
            out_specs=(vmem, vmem),
            scratch_shapes=scratch + sems,
            compiler_params=params,
        )(*keeps, window, code)
        sums = sums + lax.ppermute(sums, "row", swap)
        sums = sums + lax.ppermute(sums, "layer", swap)
        total_rows = rows * lax.axis_size("row") * lax.axis_size("layer")
        return square * (1.0 / (sums / total_rows + 1e-6))

    placed = (
        P("row", "layer", "col"),
        P("row", "layer", "col", None, None),
        P("layer", "row", "col"),
    )
    return jax.shard_map(body, mesh=mesh, in_specs=placed, out_specs=P(("row", "layer"), "col"), check_vma=False)
```

```python
import functools

import jax
import jax.numpy as jnp
from jax import lax
from jax.experimental import pallas as pl
from jax.experimental.pallas import tpu as pltpu
from jax.sharding import PartitionSpec as P

CODE_SPAN = 250.0
CODE_MID = 125.0
LOG2E = 1.4426950408889634
ID_ROWS = 16
VMEM_BYTES = 24 * 1024 * 1024
PLAN = ("S1", "K1", "S=W", "S2", "K2", "J", "S=W", "Sf2", "S3", "S=K", "Kf2", "K3")
PLACE_LIMIT = 24 << 20


def pack_kernel(cols_ref, vals_ref, *refs):
    outs, sems = refs[:-1], refs[-1]
    rows = outs[0].shape[0] - ID_ROWS
    block = vals_ref.shape[1]
    layer = lax.axis_index("layer")
    copies = []
    for k, out in enumerate(outs):
        part = 1 - layer if k < len(outs) // 2 else layer
        copies.append(
            pltpu.make_async_copy(
                vals_ref.at[pl.ds(pl.multiple_of(part * rows, block), rows)],
                out.at[pl.ds(0, rows)],
                sems.at[k],
            )
        )
        copies[-1].start()
    line = cols_ref[...].astype(jnp.float32).astype(jnp.bfloat16)
    for out in outs:
        out[rows : rows + ID_ROWS, 0 : line.shape[1]] = jnp.broadcast_to(line, (ID_ROWS, line.shape[1]))
    for copy in copies:
        copy.wait()


def place_kernel(mine, part_ref, *refs):
    window_ref, sem = refs[-2:]
    half = part_ref.shape[0]
    row = lax.axis_index("row")
    where = pl.ds(pl.multiple_of((row if mine else 1 - row) * half, half), half)
    copy = pltpu.make_async_copy(part_ref, window_ref.at[where], sem)
    copy.start()
    copy.wait()


def products(part, items, window, ids_v, ids_s, sem, finish):
    block = items[0].shape[1]
    rows = items[0].shape[0] - ID_ROWS
    live_end = window.shape[0] // block
    for s, item in enumerate(items):
        ids_v[pl.ds(s, 1)] = item[rows : rows + 1, :].astype(jnp.float32).astype(jnp.int32)
    to_scalar = pltpu.make_async_copy(ids_v, ids_s, sem)
    to_scalar.start()
    to_scalar.wait()
    for j in range(rows // block):
        left, right = [], []
        for s in range(len(items)):
            col = ids_s[s, part * (rows // block) + j]
            live = jnp.where(col < live_end, 1.0, 0.0).astype(jnp.float32)
            piece = items[s][j * block : (j + 1) * block, :]
            left.append((piece.astype(jnp.float32) * live).astype(jnp.bfloat16))
            at = pl.multiple_of(jnp.minimum(col, live_end - 1) * block, block)
            right.append(window[pl.ds(at, block), :])
        finish(
            j,
            jnp.dot(
                jnp.concatenate(left, axis=1),
                jnp.concatenate(right, axis=0),
                preferred_element_type=jnp.float32,
            ),
        )


def send_kernel(slots, *refs):
    items, (window, code_ref, ids_v, ids_s, total, sem) = refs[:slots], refs[slots:]
    block = items[0].shape[1]
    rows = total.shape[0]

    def finish(j, value):
        total[j * block : (j + 1) * block, :] = value

    products(1 - lax.axis_index("layer"), items, window, ids_v, ids_s, sem, finish)
    most = jnp.max(jnp.abs(total[...]), axis=0, keepdims=True)
    scale = (most * 1.01 + 1e-30).astype(jnp.bfloat16)
    inverse = CODE_SPAN / scale.astype(jnp.float32)
    for j in range(rows // block):
        value = total[j * block : (j + 1) * block, :]
        size = jnp.exp((jnp.abs(value) * inverse - CODE_MID) * (1.0 / LOG2E))
        code_ref[j * block : (j + 1) * block, :] = jnp.where(value < 0, -size, size).astype(jnp.bfloat16)
    code_ref[rows : rows + ID_ROWS, :] = jnp.broadcast_to(scale, (ID_ROWS, scale.shape[1]))


def keep_kernel(slots, *refs):
    items, (window, code_ref, square_ref, sum_ref, ids_v, ids_s, sem) = refs[:slots], refs[slots:]
    block = items[0].shape[1]
    rows = square_ref.shape[0]
    scale = code_ref[rows : rows + 1, :].astype(jnp.float32) * (1.0 / CODE_SPAN)
    sums = []

    def finish(j, value):
        code = code_ref[j * block : (j + 1) * block, :].astype(jnp.float32)
        size = (jnp.log(jnp.abs(code)) * LOG2E + CODE_MID) * scale
        full = value + jnp.where(code < 0, -size, size)
        square = full * full
        square_ref[j * block : (j + 1) * block, :] = square
        sums.append(jnp.sum(square, axis=0, keepdims=True))

    products(lax.axis_index("layer"), items, window, ids_v, ids_s, sem, finish)
    sum_ref[...] = functools.reduce(jnp.add, sums)


def ring_of(mesh):
    size = mesh.shape["col"]
    if size != 8:
        return list(range(size))
    return [0, 2, 4, 6, 7, 5, 3, 1]


def solution(mesh):
    size = mesh.shape["col"]
    order = ring_of(mesh)
    def shift(hops):
        return [(order[i], order[(i + hops) % size]) for i in range(size)]

    swap = [(0, 1), (1, 0)]
    vmem = pl.BlockSpec(memory_space=pltpu.VMEM)
    anywhere = pl.BlockSpec(memory_space=pl.ANY)

    def gather_two(send, keep, window, join):
        streams = {"S": [send[2]], "K": [keep[2]]}
        ends = {"S": send[:2], "K": keep[:2]}

        def move(name):
            kind = name[0]
            items = streams[kind]
            if name[1] == "f":
                hops = int(name[2])
                front, rear = ends[kind]
                src = front if kind == "S" else rear
                items.append(lax.ppermute(src, "col", shift(hops if kind == "S" else -hops)))
                return
            front, rear = ends[kind]
            front = lax.ppermute(front, "col", shift(1))
            rear = lax.ppermute(rear, "col", shift(-1))
            items.extend((front, rear))
            ends[kind] = (front, rear)

        def tie(*names):
            nonlocal window
            values = lax.optimization_barrier(tuple(window if n == "W" else (ends[n], streams[n][-1]) for n in names))
            for n, v in zip(names, values):
                if n == "W":
                    window = v
                else:
                    ends[n] = v[0]
                    streams[n][-1] = v[1]

        for name in PLAN:
            if name == "J":
                window = join(window)
            elif "=" in name:
                tie(*name.split("="))
            else:
                move(name)
        return streams["S"], streams["K"], window

    def gather_all(item):
        stacked = lax.all_gather(item, "col", axis=0)
        return [stacked[i] for i in range(size)]

    def body(flow_cols, flow_vals, window_flow):
        block = flow_vals.shape[-1]
        count = flow_vals.shape[0] // 2
        rows = count * block
        own = window_flow[0]
        half, columns = own.shape
        other = lax.ppermute(own, "row", swap)
        item = jax.ShapeDtypeStruct((rows + ID_ROWS, block), flow_vals.dtype)
        params = pltpu.CompilerParams(vmem_limit_bytes=VMEM_BYTES)
        items = pl.pallas_call(
            pack_kernel,
            out_shape=(item,) * 2,
            in_specs=[vmem, anywhere],
            out_specs=(vmem,) * 2,
            scratch_shapes=[pltpu.SemaphoreType.DMA((2,))],
            compiler_params=params,
        )(flow_cols.reshape(1, 2 * count), flow_vals.reshape(2 * rows, block))
        send, keep = items[:1] * 3, items[1:] * 3

        def place(mine, part, window=None):
            given = [] if window is None else [window]
            return pl.pallas_call(
                functools.partial(place_kernel, mine),
                out_shape=jax.ShapeDtypeStruct((2 * half, columns), own.dtype),
                in_specs=[anywhere] + [vmem] * len(given),
                out_specs=vmem,
                scratch_shapes=[pltpu.SemaphoreType.DMA(())],
                input_output_aliases={1: 0} if given else {},
                compiler_params=pltpu.CompilerParams(vmem_limit_bytes=PLACE_LIMIT),
                cost_estimate=pl.CostEstimate(flops=0, bytes_accessed=2 * half * columns * 2, transcendentals=0),
            )(part, *given)

        window = place(True, own)
        if size == 8:
            sends, keeps, window = gather_two(send, keep, window, lambda w: place(False, other, w))
        else:
            sends, keeps = gather_all(send[0]), gather_all(keep[0])
            window = place(False, other, window)
        scratch = [
            pltpu.VMEM((max(size, 8), block), jnp.int32),
            pltpu.SMEM((max(size, 8), block), jnp.int32),
        ]
        sems = [pltpu.SemaphoreType.DMA(())]
        item_specs = [vmem] * size
        code = pl.pallas_call(
            functools.partial(send_kernel, size),
            out_shape=jax.ShapeDtypeStruct((rows + ID_ROWS, columns), jnp.bfloat16),
            in_specs=item_specs + [vmem],
            out_specs=vmem,
            scratch_shapes=scratch + [pltpu.VMEM((rows, columns), jnp.float32)] + sems,
            compiler_params=params,
        )(*sends, window)
        code = lax.ppermute(code, "layer", swap)
        square, sums = pl.pallas_call(
            functools.partial(keep_kernel, size),
            out_shape=(
                jax.ShapeDtypeStruct((rows, columns), jnp.float32),
                jax.ShapeDtypeStruct((1, columns), jnp.float32),
            ),
            in_specs=item_specs + [vmem, vmem],
            out_specs=(vmem, vmem),
            scratch_shapes=scratch + sems,
            compiler_params=params,
        )(*keeps, window, code)
        sums = sums + lax.ppermute(sums, "row", swap)
        sums = sums + lax.ppermute(sums, "layer", swap)
        total_rows = rows * lax.axis_size("row") * lax.axis_size("layer")
        return square * (1.0 / (sums / total_rows + 1e-6))

    placed = (
        P("row", "layer", "col"),
        P("row", "layer", "col", None, None),
        P("layer", "row", "col"),
    )
    return jax.shard_map(body, mesh=mesh, in_specs=placed, out_specs=P(("row", "layer"), "col"), check_vma=False)
```

```python
import functools

import jax
import jax.numpy as jnp
from jax import lax
from jax.experimental import pallas as pl
from jax.experimental.pallas import tpu as pltpu
from jax.sharding import PartitionSpec as P

CODE_SPAN = 250.0
CODE_MID = 125.0
LOG2E = 1.4426950408889634
ID_ROWS = 16
VMEM_BYTES = 24 * 1024 * 1024
PACK_LIMIT = 24 << 20
PLAN = ("S=K=T", "O", "S1", "K1", "S=W", "S2", "K2", "J", "S=W", "Sf2", "S3", "S=K", "C", "X", "Kf2", "K3")
PLACE_LIMIT = 24 << 20


def pack_kernel(cols_ref, vals_ref, *refs):
    outs, sems = refs[:-1], refs[-1]
    rows = outs[0].shape[0] - ID_ROWS
    block = vals_ref.shape[1]
    layer = lax.axis_index("layer")
    copies = []
    for k, out in enumerate(outs):
        part = 1 - layer if k < len(outs) // 2 else layer
        copies.append(
            pltpu.make_async_copy(
                vals_ref.at[pl.ds(pl.multiple_of(part * rows, block), rows)],
                out.at[pl.ds(0, rows)],
                sems.at[k],
            )
        )
        copies[-1].start()
    line = cols_ref[...].astype(jnp.float32).astype(jnp.bfloat16)
    for out in outs:
        out[rows : rows + ID_ROWS, 0 : line.shape[1]] = jnp.broadcast_to(line, (ID_ROWS, line.shape[1]))
    for copy in copies:
        copy.wait()


def place_kernel(mine, part_ref, *refs):
    window_ref, sem = refs[-2:]
    half = part_ref.shape[0]
    row = lax.axis_index("row")
    where = pl.ds(pl.multiple_of((row if mine else 1 - row) * half, half), half)
    copy = pltpu.make_async_copy(part_ref, window_ref.at[where], sem)
    copy.start()
    copy.wait()


def products(part, items, window, ids_v, ids_s, sem, finish):
    block = items[0].shape[1]
    rows = items[0].shape[0] - ID_ROWS
    live_end = window.shape[0] // block
    for s, item in enumerate(items):
        ids_v[pl.ds(s, 1)] = item[rows : rows + 1, :].astype(jnp.float32).astype(jnp.int32)
    to_scalar = pltpu.make_async_copy(ids_v, ids_s, sem)
    to_scalar.start()
    to_scalar.wait()
    for j in range(rows // block):
        left, right = [], []
        for s in range(len(items)):
            col = ids_s[s, part * (rows // block) + j]
            live = jnp.where(col < live_end, 1.0, 0.0).astype(jnp.float32)
            piece = items[s][j * block : (j + 1) * block, :]
            left.append((piece.astype(jnp.float32) * live).astype(jnp.bfloat16))
            at = pl.multiple_of(jnp.minimum(col, live_end - 1) * block, block)
            right.append(window[pl.ds(at, block), :])
        finish(
            j,
            jnp.dot(
                jnp.concatenate(left, axis=1),
                jnp.concatenate(right, axis=0),
                preferred_element_type=jnp.float32,
            ),
        )


def send_kernel(slots, *refs):
    items, (window, code_ref, ids_v, ids_s, total, sem) = refs[:slots], refs[slots:]
    block = items[0].shape[1]
    rows = total.shape[0]

    def finish(j, value):
        total[j * block : (j + 1) * block, :] = value

    products(1 - lax.axis_index("layer"), items, window, ids_v, ids_s, sem, finish)
    most = jnp.max(jnp.abs(total[...]), axis=0, keepdims=True)
    scale = (most * 1.01 + 1e-30).astype(jnp.bfloat16)
    inverse = CODE_SPAN / scale.astype(jnp.float32)
    for j in range(rows // block):
        value = total[j * block : (j + 1) * block, :]
        size = jnp.exp((jnp.abs(value) * inverse - CODE_MID) * (1.0 / LOG2E))
        code_ref[j * block : (j + 1) * block, :] = jnp.where(value < 0, -size, size).astype(jnp.bfloat16)
    code_ref[rows : rows + ID_ROWS, :] = jnp.broadcast_to(scale, (ID_ROWS, scale.shape[1]))


def keep_kernel(slots, *refs):
    items, (window, code_ref, square_ref, sum_ref, ids_v, ids_s, sem) = refs[:slots], refs[slots:]
    block = items[0].shape[1]
    rows = square_ref.shape[0]
    scale = code_ref[rows : rows + 1, :].astype(jnp.float32) * (1.0 / CODE_SPAN)
    sums = []

    def finish(j, value):
        code = code_ref[j * block : (j + 1) * block, :].astype(jnp.float32)
        size = (jnp.log(jnp.abs(code)) * LOG2E + CODE_MID) * scale
        full = value + jnp.where(code < 0, -size, size)
        square = full * full
        square_ref[j * block : (j + 1) * block, :] = square
        sums.append(jnp.sum(square, axis=0, keepdims=True))

    products(lax.axis_index("layer"), items, window, ids_v, ids_s, sem, finish)
    sum_ref[...] = functools.reduce(jnp.add, sums)


def ring_of(mesh):
    size = mesh.shape["col"]
    if size != 8:
        return list(range(size))
    return [0, 2, 4, 6, 7, 5, 3, 1]


def solution(mesh):
    size = mesh.shape["col"]
    order = ring_of(mesh)
    def shift(hops):
        return [(order[i], order[(i + hops) % size]) for i in range(size)]

    swap = [(0, 1), (1, 0)]
    vmem = pl.BlockSpec(memory_space=pltpu.VMEM)
    anywhere = pl.BlockSpec(memory_space=pl.ANY)

    def gather_all(item):
        stacked = lax.all_gather(item, "col", axis=0)
        return [stacked[i] for i in range(size)]

    def body(flow_cols, flow_vals, window_flow):
        block = flow_vals.shape[-1]
        count = flow_vals.shape[0] // 2
        rows = count * block
        own = window_flow[0]
        half, columns = own.shape
        item = jax.ShapeDtypeStruct((rows + ID_ROWS, block), flow_vals.dtype)
        params = pltpu.CompilerParams(vmem_limit_bytes=VMEM_BYTES)
        items = pl.pallas_call(
            pack_kernel,
            out_shape=(item,) * 2,
            in_specs=[vmem, anywhere],
            out_specs=(vmem,) * 2,
            scratch_shapes=[pltpu.SemaphoreType.DMA((2,))],
            compiler_params=pltpu.CompilerParams(vmem_limit_bytes=PACK_LIMIT),
        )(flow_cols.reshape(1, 2 * count), flow_vals.reshape(2 * rows, block))
        theirs = own
        send, keep = items[:1] * 3, items[1:] * 3

        def place(mine, part, window=None):
            given = [] if window is None else [window]
            return pl.pallas_call(
                functools.partial(place_kernel, mine),
                out_shape=jax.ShapeDtypeStruct((2 * half, columns), own.dtype),
                in_specs=[anywhere] + [vmem] * len(given),
                out_specs=vmem,
                scratch_shapes=[pltpu.SemaphoreType.DMA(())],
                input_output_aliases={1: 0} if given else {},
                compiler_params=pltpu.CompilerParams(vmem_limit_bytes=PLACE_LIMIT),
                cost_estimate=pl.CostEstimate(flops=0, bytes_accessed=2 * half * columns * 2, transcendentals=0),
            )(part, *given)

        scratch = [
            pltpu.VMEM((max(size, 8), block), jnp.int32),
            pltpu.SMEM((max(size, 8), block), jnp.int32),
        ]
        sems = [pltpu.SemaphoreType.DMA(())]
        item_specs = [vmem] * size

        def coded(sends, window):
            return pl.pallas_call(
                functools.partial(send_kernel, size),
                out_shape=jax.ShapeDtypeStruct((rows + ID_ROWS, columns), jnp.bfloat16),
                in_specs=item_specs + [vmem],
                out_specs=vmem,
                scratch_shapes=scratch + [pltpu.VMEM((rows, columns), jnp.float32)] + sems,
                compiler_params=params,
            )(*sends, window)

        window = place(True, own)
        if size == 8:
            ends = {"S": (send[0], send[0]), "K": (keep[0], keep[0])}
            lists = {"S": [send[0]], "K": [keep[0]]}
            code = other = None

            def tie(names):
                nonlocal window, code, theirs, other
                given = {"W": window, "C": code, "T": theirs, "O": other}
                for n in "SK":
                    given[n] = (ends[n], lists[n][-1])
                done = lax.optimization_barrier(tuple(given[n] for n in names))
                for n, value in zip(names, done):
                    if n == "W":
                        window = value
                    elif n == "C":
                        code = value
                    elif n == "T":
                        theirs = value
                    elif n == "O":
                        other = value
                    else:
                        ends[n], lists[n][-1] = value

            for name in PLAN:
                if name == "O":
                    other = lax.ppermute(theirs, "row", swap)
                elif name == "J":
                    window = place(False, other, window)
                elif name == "C":
                    code = coded(lists["S"], window)
                elif name == "X":
                    code = lax.ppermute(code, "layer", swap)
                elif "=" in name:
                    tie(name.split("="))
                elif name[1] == "f":
                    kind, way = (name[0], 2 if name[0] == "S" else -2)
                    lists[kind].append(lax.ppermute(ends[kind][0 if way > 0 else 1], "col", shift(way)))
                else:
                    kind = name[0]
                    ends[kind] = tuple(lax.ppermute(e, "col", shift(w)) for e, w in zip(ends[kind], (1, -1)))
                    lists[kind].extend(ends[kind])
            keeps = lists["K"]
        else:
            sends, keeps = gather_all(send[0]), gather_all(keep[0])
            window = place(False, lax.ppermute(own, "row", swap), window)
            code = lax.ppermute(coded(sends, window), "layer", swap)
        square, sums = pl.pallas_call(
            functools.partial(keep_kernel, size),
            out_shape=(
                jax.ShapeDtypeStruct((rows, columns), jnp.float32),
                jax.ShapeDtypeStruct((1, columns), jnp.float32),
            ),
            in_specs=item_specs + [vmem, vmem],
            out_specs=(vmem, vmem),
            scratch_shapes=scratch + sems,
            compiler_params=params,
        )(*keeps, window, code)
        sums = sums + lax.ppermute(sums, "row", swap)
        sums = sums + lax.ppermute(sums, "layer", swap)
        total_rows = rows * lax.axis_size("row") * lax.axis_size("layer")
        return square * (1.0 / (sums / total_rows + 1e-6))

    placed = (
        P("row", "layer", "col"),
        P("row", "layer", "col", None, None),
        P("layer", "row", "col"),
    )
    return jax.shard_map(body, mesh=mesh, in_specs=placed, out_specs=P(("row", "layer"), "col"), check_vma=False)
```

```python
import functools

import jax
import jax.numpy as jnp
from jax import lax
from jax.experimental import pallas as pl
from jax.experimental.pallas import tpu as pltpu
from jax.sharding import PartitionSpec as P

CODE_SPAN = 250.0
CODE_MID = 125.0
LOG2E = 1.4426950408889634
ID_ROWS = 16
VMEM_BYTES = 24 * 1024 * 1024
PACK_LIMIT = 24 << 20
PLAN = ("S=K=T", "O", "S1", "K1", "S=W", "S2", "K2", "J", "S=W", "Sf2", "S3", "S=K", "C", "X", "Kf2", "K3")
PLACE_LIMIT = 24 << 20


def pack_kernel(cols_ref, vals_ref, *refs):
    outs, sems = refs[:-1], refs[-1]
    rows = outs[0].shape[0] - ID_ROWS
    block = vals_ref.shape[1]
    layer = lax.axis_index("layer")
    copies = []
    for k, out in enumerate(outs):
        part = 1 - layer if k < len(outs) // 2 else layer
        copies.append(
            pltpu.make_async_copy(
                vals_ref.at[pl.ds(pl.multiple_of(part * rows, block), rows)],
                out.at[pl.ds(0, rows)],
                sems.at[k],
            )
        )
        copies[-1].start()
    line = jnp.pad(cols_ref[...], ((0, 0), (0, block - cols_ref.shape[1])))
    line = jnp.broadcast_to(line, (ID_ROWS, block)).astype(jnp.float32).astype(jnp.bfloat16)
    for out in outs:
        out[rows : rows + ID_ROWS, :] = line
    for copy in copies:
        copy.wait()


def pick_kernel(first_ref, last_ref, out_ref):
    col = lax.axis_index("col")
    odd = lax.rem(col + lax.div(col, 2), 2)

    @pl.when(odd == 0)
    def _():
        out_ref[...] = first_ref[...]

    @pl.when(odd != 0)
    def _():
        out_ref[...] = last_ref[...]


def place_kernel(mine, part_ref, *refs):
    window_ref, sem = refs[-2:]
    half = part_ref.shape[0]
    row = lax.axis_index("row")
    where = pl.ds(pl.multiple_of((row if mine else 1 - row) * half, half), half)
    copy = pltpu.make_async_copy(part_ref, window_ref.at[where], sem)
    copy.start()
    copy.wait()


def products(part, items, window, finish):
    block = items[0].shape[1]
    rows = items[0].shape[0] - ID_ROWS
    live_end = window.shape[0] // block
    lanes = lax.broadcasted_iota(jnp.int32, (1, block), 1)
    lines = [item[rows : rows + 1, :].astype(jnp.float32).astype(jnp.int32) for item in items]
    for j in range(rows // block):
        left, right = [], []
        for s in range(len(items)):
            col = jnp.sum(jnp.where(lanes == part * (rows // block) + j, lines[s], 0))
            live = jnp.where(col < live_end, 1.0, 0.0).astype(jnp.float32)
            piece = items[s][j * block : (j + 1) * block, :]
            left.append((piece.astype(jnp.float32) * live).astype(jnp.bfloat16))
            at = pl.multiple_of(jnp.minimum(col, live_end - 1) * block, block)
            right.append(window[pl.ds(at, block), :])
        finish(
            j,
            jnp.dot(
                jnp.concatenate(left, axis=1),
                jnp.concatenate(right, axis=0),
                preferred_element_type=jnp.float32,
            ),
        )


def send_kernel(slots, *refs):
    items, (window, code_ref, total) = refs[:slots], refs[slots:]
    block = items[0].shape[1]
    rows = total.shape[0]

    def finish(j, value):
        total[j * block : (j + 1) * block, :] = value

    products(1 - lax.axis_index("layer"), items, window, finish)
    most = jnp.max(jnp.abs(total[...]), axis=0, keepdims=True)
    scale = (most * 1.01 + 1e-30).astype(jnp.bfloat16)
    inverse = CODE_SPAN / scale.astype(jnp.float32)
    for j in range(rows // block):
        value = total[j * block : (j + 1) * block, :]
        size = jnp.exp((jnp.abs(value) * inverse - CODE_MID) * (1.0 / LOG2E))
        code_ref[j * block : (j + 1) * block, :] = jnp.where(value < 0, -size, size).astype(jnp.bfloat16)
    code_ref[rows : rows + ID_ROWS, :] = jnp.broadcast_to(scale, (ID_ROWS, scale.shape[1]))


def keep_kernel(slots, *refs):
    items, (window, code_ref, square_ref, sum_ref) = refs[:slots], refs[slots:]
    block = items[0].shape[1]
    rows = square_ref.shape[0]
    scale = code_ref[rows : rows + 1, :].astype(jnp.float32) * (1.0 / CODE_SPAN)
    sums = []

    def finish(j, value):
        code = code_ref[j * block : (j + 1) * block, :].astype(jnp.float32)
        size = (jnp.log(jnp.abs(code)) * LOG2E + CODE_MID) * scale
        full = value + jnp.where(code < 0, -size, size)
        square = full * full
        square_ref[j * block : (j + 1) * block, :] = square
        sums.append(jnp.sum(square, axis=0, keepdims=True))

    products(lax.axis_index("layer"), items, window, finish)
    sum_ref[...] = functools.reduce(jnp.add, sums)


def ring_of(mesh):
    size = mesh.shape["col"]
    if size != 8:
        return list(range(size))
    return [0, 2, 4, 6, 7, 5, 3, 1]


def solution(mesh):
    size = mesh.shape["col"]
    order = ring_of(mesh)
    def shift(hops):
        return [(order[i], order[(i + hops) % size]) for i in range(size)]

    swap = [(0, 1), (1, 0)]
    vmem = pl.BlockSpec(memory_space=pltpu.VMEM)
    anywhere = pl.BlockSpec(memory_space=pl.ANY)

    across = [(order[a], order[b]) for a, b in ((6, 1), (5, 2), (2, 5), (1, 6), (3, 0), (0, 3), (7, 4), (4, 7))] if size == 8 else []

    def gather_all(item):
        stacked = lax.all_gather(item, "col", axis=0)
        return [stacked[i] for i in range(size)]

    def body(flow_cols, flow_vals, window_flow):
        block = flow_vals.shape[-1]
        count = flow_vals.shape[0] // 2
        rows = count * block
        own = window_flow[0]
        half, columns = own.shape
        item = jax.ShapeDtypeStruct((rows + ID_ROWS, block), flow_vals.dtype)
        params = pltpu.CompilerParams(vmem_limit_bytes=VMEM_BYTES)
        items = pl.pallas_call(
            pack_kernel,
            out_shape=(item,) * 2,
            in_specs=[vmem, anywhere],
            out_specs=(vmem,) * 2,
            scratch_shapes=[pltpu.SemaphoreType.DMA((2,))],
            compiler_params=pltpu.CompilerParams(vmem_limit_bytes=PACK_LIMIT),
        )(flow_cols.reshape(1, 2 * count), flow_vals.reshape(2 * rows, block))
        theirs = own
        send, keep = items[:1] * 3, items[1:] * 3

        def pick(first, last):
            return pl.pallas_call(
                pick_kernel, out_shape=item, in_specs=[vmem, vmem], out_specs=vmem, compiler_params=params
            )(first, last)

        def place(mine, part, window=None):
            given = [] if window is None else [window]
            return pl.pallas_call(
                functools.partial(place_kernel, mine),
                out_shape=jax.ShapeDtypeStruct((2 * half, columns), own.dtype),
                in_specs=[anywhere] + [vmem] * len(given),
                out_specs=vmem,
                scratch_shapes=[pltpu.SemaphoreType.DMA(())],
                input_output_aliases={1: 0} if given else {},
                compiler_params=pltpu.CompilerParams(vmem_limit_bytes=PLACE_LIMIT),
                cost_estimate=pl.CostEstimate(flops=0, bytes_accessed=2 * half * columns * 2, transcendentals=0),
            )(part, *given)

        item_specs = [vmem] * size

        def coded(sends, window):
            return pl.pallas_call(
                functools.partial(send_kernel, size),
                out_shape=jax.ShapeDtypeStruct((rows + ID_ROWS, columns), jnp.bfloat16),
                in_specs=item_specs + [vmem],
                out_specs=vmem,
                scratch_shapes=[pltpu.VMEM((rows, columns), jnp.float32)],
                compiler_params=params,
            )(*sends, window)

        window = place(True, own)
        if size == 8:
            chosen = {}
            ends = {"S": (send[0], send[0]), "K": (keep[0], keep[0])}
            lists = {"S": [send[0]], "K": [keep[0]]}
            code = other = None

            def tie(names):
                nonlocal window, code, theirs, other
                given = {"W": window, "C": code, "T": theirs, "O": other}
                for n in "SK":
                    given[n] = (ends[n], lists[n][-1])
                    given[n + "p"] = chosen.get(n)
                done = lax.optimization_barrier(tuple(given[n] for n in names))
                for n, value in zip(names, done):
                    if n == "W":
                        window = value
                    elif n == "C":
                        code = value
                    elif n[-1] == "p":
                        chosen[n[0]] = value
                    elif n == "T":
                        theirs = value
                    elif n == "O":
                        other = value
                    else:
                        ends[n], lists[n][-1] = value

            for name in PLAN:
                if name == "O":
                    other = lax.ppermute(theirs, "row", swap)
                elif name == "J":
                    window = place(False, other, window)
                elif name == "C":
                    code = coded(lists["S"], window)
                elif name == "X":
                    code = lax.ppermute(code, "layer", swap)
                elif "=" in name:
                    tie(name.split("="))
                elif name[1] == "f":
                    kind, way = (name[0], 2 if name[0] == "S" else -2)
                    lists[kind].append(lax.ppermute(ends[kind][0 if way > 0 else 1], "col", shift(way)))
                elif name[1] == "p":
                    chosen[name[0]] = pick(*ends[name[0]])
                elif name[1] == "m":
                    lists[name[0]].append(lax.ppermute(chosen[name[0]], "col", across))
                else:
                    kind = name[0]
                    ends[kind] = tuple(lax.ppermute(e, "col", shift(w)) for e, w in zip(ends[kind], (1, -1)))
                    lists[kind].extend(ends[kind])
            keeps = lists["K"]
        else:
            sends, keeps = gather_all(send[0]), gather_all(keep[0])
            window = place(False, lax.ppermute(own, "row", swap), window)
            code = lax.ppermute(coded(sends, window), "layer", swap)
        square, sums = pl.pallas_call(
            functools.partial(keep_kernel, size),
            out_shape=(
                jax.ShapeDtypeStruct((rows, columns), jnp.float32),
                jax.ShapeDtypeStruct((1, columns), jnp.float32),
            ),
            in_specs=item_specs + [vmem, vmem],
            out_specs=(vmem, vmem),
            compiler_params=params,
        )(*keeps, window, code)
        sums = sums + lax.ppermute(sums, "row", swap)
        sums = sums + lax.ppermute(sums, "layer", swap)
        total_rows = rows * lax.axis_size("row") * lax.axis_size("layer")
        return square * (1.0 / (sums / total_rows + 1e-6))

    placed = (
        P("row", "layer", "col"),
        P("row", "layer", "col", None, None),
        P("layer", "row", "col"),
    )
    return jax.shard_map(body, mesh=mesh, in_specs=placed, out_specs=P(("row", "layer"), "col"), check_vma=False)
```

```python
import functools

import jax
import jax.numpy as jnp
from jax import lax
from jax.experimental import pallas as pl
from jax.experimental.pallas import tpu as pltpu
from jax.sharding import PartitionSpec as P

CODE_SPAN = 250.0
CODE_MID = 125.0
LOG2E = 1.4426950408889634
ID_ROWS = 16
VMEM_BYTES = 24 * 1024 * 1024
PLAN = ("S=K=T", "O", "S1", "K1", "S=W", "Sp", "Kp", "S2", "K2", "J", "S=W=Sp=Kp", "S3", "Sm", "S=K", "C", "X", "K3", "Km")


def pack_kernel(cols_ref, vals_ref, *refs):
    outs, sems = refs[:-1], refs[-1]
    rows = outs[0].shape[0] - ID_ROWS
    block = vals_ref.shape[1]
    layer = lax.axis_index("layer")
    copies = []
    for k, out in enumerate(outs):
        part = 1 - layer if k < len(outs) // 2 else layer
        copies.append(
            pltpu.make_async_copy(
                vals_ref.at[pl.ds(pl.multiple_of(part * rows, block), rows)],
                out.at[pl.ds(0, rows)],
                sems.at[k],
            )
        )
        copies[-1].start()
    line = jnp.pad(cols_ref[...], ((0, 0), (0, block - cols_ref.shape[1])))
    line = jnp.broadcast_to(line, (ID_ROWS, block)).astype(jnp.float32).astype(jnp.bfloat16)
    for out in outs:
        out[rows : rows + ID_ROWS, :] = line
    for copy in copies:
        copy.wait()


def pick_kernel(first_ref, last_ref, out_ref):
    col = lax.axis_index("col")
    odd = lax.rem(col + lax.div(col, 2), 2)

    @pl.when(odd == 0)
    def _():
        out_ref[...] = first_ref[...]

    @pl.when(odd != 0)
    def _():
        out_ref[...] = last_ref[...]


def place_kernel(mine, part_ref, *refs):
    window_ref, sem = refs[-2:]
    half = part_ref.shape[0]
    row = lax.axis_index("row")
    where = pl.ds(pl.multiple_of((row if mine else 1 - row) * half, half), half)
    copy = pltpu.make_async_copy(part_ref, window_ref.at[where], sem)
    copy.start()
    copy.wait()


def products(part, items, window, finish):
    block = items[0].shape[1]
    rows = items[0].shape[0] - ID_ROWS
    live_end = window.shape[0] // block
    lanes = lax.broadcasted_iota(jnp.int32, (1, block), 1)
    lines = [item[rows : rows + 1, :].astype(jnp.float32).astype(jnp.int32) for item in items]
    for j in range(rows // block):
        left, right = [], []
        for s in range(len(items)):
            col = jnp.sum(jnp.where(lanes == part * (rows // block) + j, lines[s], 0))
            live = jnp.where(col < live_end, 1.0, 0.0).astype(jnp.float32)
            piece = items[s][j * block : (j + 1) * block, :]
            left.append((piece.astype(jnp.float32) * live).astype(jnp.bfloat16))
            at = pl.multiple_of(jnp.minimum(col, live_end - 1) * block, block)
            right.append(window[pl.ds(at, block), :])
        finish(
            j,
            jnp.dot(
                jnp.concatenate(left, axis=1),
                jnp.concatenate(right, axis=0),
                preferred_element_type=jnp.float32,
            ),
        )


def send_kernel(slots, *refs):
    items, (window, code_ref, total) = refs[:slots], refs[slots:]
    block = items[0].shape[1]
    rows = total.shape[0]

    def finish(j, value):
        total[j * block : (j + 1) * block, :] = value

    products(1 - lax.axis_index("layer"), items, window, finish)
    most = jnp.max(jnp.abs(total[...]), axis=0, keepdims=True)
    scale = (most * 1.01 + 1e-30).astype(jnp.bfloat16)
    inverse = CODE_SPAN / scale.astype(jnp.float32)
    for j in range(rows // block):
        value = total[j * block : (j + 1) * block, :]
        size = jnp.exp((jnp.abs(value) * inverse - CODE_MID) * (1.0 / LOG2E))
        code_ref[j * block : (j + 1) * block, :] = jnp.where(value < 0, -size, size).astype(jnp.bfloat16)
    code_ref[rows : rows + ID_ROWS, :] = jnp.broadcast_to(scale, (ID_ROWS, scale.shape[1]))


def keep_kernel(slots, *refs):
    items, (window, code_ref, square_ref, sum_ref) = refs[:slots], refs[slots:]
    block = items[0].shape[1]
    rows = square_ref.shape[0]
    scale = code_ref[rows : rows + 1, :].astype(jnp.float32) * (1.0 / CODE_SPAN)
    sums = []

    def finish(j, value):
        code = code_ref[j * block : (j + 1) * block, :].astype(jnp.float32)
        size = (jnp.log(jnp.abs(code)) * LOG2E + CODE_MID) * scale
        full = value + jnp.where(code < 0, -size, size)
        square = full * full
        square_ref[j * block : (j + 1) * block, :] = square
        sums.append(jnp.sum(square, axis=0, keepdims=True))

    products(lax.axis_index("layer"), items, window, finish)
    sum_ref[...] = functools.reduce(jnp.add, sums)


def solution(mesh):
    size = mesh.shape["col"]
    ring = [0, 2, 4, 6, 7, 5, 3, 1]
    across = [(ring[a], ring[b]) for a, b in ((6, 1), (5, 2), (2, 5), (1, 6), (3, 0), (0, 3), (7, 4), (4, 7))]

    def shift(hops):
        return [(ring[i], ring[(i + hops) % len(ring)]) for i in range(len(ring))]

    swap = [(0, 1), (1, 0)]
    vmem = pl.BlockSpec(memory_space=pltpu.VMEM)
    anywhere = pl.BlockSpec(memory_space=pl.ANY)

    def gather_all(item):
        stacked = lax.all_gather(item, "col", axis=0)
        return [stacked[i] for i in range(size)]

    def body(flow_cols, flow_vals, window_flow):
        block = flow_vals.shape[-1]
        count = flow_vals.shape[0] // 2
        rows = count * block
        own = window_flow[0]
        half, columns = own.shape
        item = jax.ShapeDtypeStruct((rows + ID_ROWS, block), flow_vals.dtype)
        params = pltpu.CompilerParams(vmem_limit_bytes=VMEM_BYTES)
        items = pl.pallas_call(
            pack_kernel,
            out_shape=(item,) * 2,
            in_specs=[vmem, anywhere],
            out_specs=(vmem,) * 2,
            scratch_shapes=[pltpu.SemaphoreType.DMA((2,))],
            compiler_params=params,
        )(flow_cols.reshape(1, 2 * count), flow_vals.reshape(2 * rows, block))
        theirs = own
        send, keep = items[:1] * 3, items[1:] * 3

        def pick(first, last):
            return pl.pallas_call(
                pick_kernel, out_shape=item, in_specs=[vmem, vmem], out_specs=vmem, compiler_params=params
            )(first, last)

        def place(mine, part, window=None):
            given = [] if window is None else [window]
            return pl.pallas_call(
                functools.partial(place_kernel, mine),
                out_shape=jax.ShapeDtypeStruct((2 * half, columns), own.dtype),
                in_specs=[anywhere] + [vmem] * len(given),
                out_specs=vmem,
                scratch_shapes=[pltpu.SemaphoreType.DMA(())],
                input_output_aliases={1: 0} if given else {},
                compiler_params=params,
                cost_estimate=pl.CostEstimate(flops=0, bytes_accessed=2 * half * columns * 2, transcendentals=0),
            )(part, *given)

        item_specs = [vmem] * size

        def coded(sends, window):
            return pl.pallas_call(
                functools.partial(send_kernel, size),
                out_shape=jax.ShapeDtypeStruct((rows + ID_ROWS, columns), jnp.bfloat16),
                in_specs=item_specs + [vmem],
                out_specs=vmem,
                scratch_shapes=[pltpu.VMEM((rows, columns), jnp.float32)],
                compiler_params=params,
            )(*sends, window)

        window = place(True, own)
        if size == 8:
            chosen = {}
            ends = {"S": (send[0], send[0]), "K": (keep[0], keep[0])}
            lists = {"S": [send[0]], "K": [keep[0]]}
            code = other = None

            def tie(names):
                nonlocal window, code, theirs, other
                given = {"W": window, "C": code, "T": theirs, "O": other}
                for n in "SK":
                    given[n] = (ends[n], lists[n][-1])
                    given[n + "p"] = chosen.get(n)
                done = lax.optimization_barrier(tuple(given[n] for n in names))
                for n, value in zip(names, done):
                    if n == "W":
                        window = value
                    elif n == "C":
                        code = value
                    elif n[-1] == "p":
                        chosen[n[0]] = value
                    elif n == "T":
                        theirs = value
                    elif n == "O":
                        other = value
                    else:
                        ends[n], lists[n][-1] = value

            for name in PLAN:
                if name == "O":
                    other = lax.ppermute(theirs, "row", swap)
                elif name == "J":
                    window = place(False, other, window)
                elif name == "C":
                    code = coded(lists["S"], window)
                elif name == "X":
                    code = lax.ppermute(code, "layer", swap)
                elif "=" in name:
                    tie(name.split("="))
                elif name[1] == "p":
                    chosen[name[0]] = pick(*ends[name[0]])
                elif name[1] == "m":
                    lists[name[0]].append(lax.ppermute(chosen[name[0]], "col", across))
                else:
                    kind = name[0]
                    ends[kind] = tuple(lax.ppermute(e, "col", shift(w)) for e, w in zip(ends[kind], (1, -1)))
                    lists[kind].extend(ends[kind])
            keeps = lists["K"]
        else:
            sends, keeps = gather_all(send[0]), gather_all(keep[0])
            window = place(False, lax.ppermute(own, "row", swap), window)
            code = lax.ppermute(coded(sends, window), "layer", swap)
        square, sums = pl.pallas_call(
            functools.partial(keep_kernel, size),
            out_shape=(
                jax.ShapeDtypeStruct((rows, columns), jnp.float32),
                jax.ShapeDtypeStruct((1, columns), jnp.float32),
            ),
            in_specs=item_specs + [vmem, vmem],
            out_specs=(vmem, vmem),
            compiler_params=params,
        )(*keeps, window, code)
        cross = [(0, 3), (1, 2), (2, 1), (3, 0)]
        sums = sums + lax.ppermute(sums, "row", swap) + lax.ppermute(sums, "layer", swap) + lax.ppermute(sums, ("row", "layer"), cross)
        total_rows = rows * lax.axis_size("row") * lax.axis_size("layer")
        return square * (1.0 / (sums / total_rows + 1e-6))

    placed = (
        P("row", "layer", "col"),
        P("row", "layer", "col", None, None),
        P("layer", "row", "col"),
    )
    return jax.shard_map(body, mesh=mesh, in_specs=placed, out_specs=P(("row", "layer"), "col"), check_vma=False)
```

```python
import functools

import jax
import jax.numpy as jnp
from jax import lax
from jax.experimental import pallas as pl
from jax.experimental.pallas import tpu as pltpu
from jax.sharding import PartitionSpec as P

CODE_SPAN = 250.0
CODE_MID = 125.0
LOG2E = 1.4426950408889634
ID_ROWS = 16
VMEM_BYTES = 24 * 1024 * 1024
PLAN = ("S=K=T", "O", "S1", "K1", "S=W", "Sp", "Kp", "S2", "K2", "J", "S=W=Sp=Kp", "S3", "Sm", "S=K", "C", "X", "K3", "Km")


def pack_kernel(cols_ref, vals_ref, *refs):
    outs, sems = refs[:-1], refs[-1]
    rows = outs[0].shape[0] - ID_ROWS
    block = vals_ref.shape[1]
    layer = lax.axis_index("layer")
    copies = []
    for k, out in enumerate(outs):
        part = 1 - layer if k < len(outs) // 2 else layer
        copies.append(
            pltpu.make_async_copy(
                vals_ref.at[pl.ds(pl.multiple_of(part * rows, block), rows)],
                out.at[pl.ds(0, rows)],
                sems.at[k],
            )
        )
        copies[-1].start()
    line = jnp.pad(cols_ref[...], ((0, 0), (0, block - cols_ref.shape[1])))
    line = jnp.broadcast_to(line, (ID_ROWS, block)).astype(jnp.float32).astype(jnp.bfloat16)
    for out in outs:
        out[rows : rows + ID_ROWS, :] = line
    for copy in copies:
        copy.wait()


def pick_kernel(first_ref, last_ref, out_ref):
    col = lax.axis_index("col")
    odd = lax.rem(col + lax.div(col, 2) + 1, 2)

    @pl.when(odd == 0)
    def _():
        out_ref[...] = first_ref[...]

    @pl.when(odd != 0)
    def _():
        out_ref[...] = last_ref[...]


def place_kernel(mine, part_ref, *refs):
    window_ref, sem = refs[-2:]
    half = part_ref.shape[0]
    row = lax.axis_index("row")
    where = pl.ds(pl.multiple_of((row if mine else 1 - row) * half, half), half)
    copy = pltpu.make_async_copy(part_ref, window_ref.at[where], sem)
    copy.start()
    copy.wait()


def products(part, items, window, finish):
    block = items[0].shape[1]
    rows = items[0].shape[0] - ID_ROWS
    live_end = window.shape[0] // block
    lanes = lax.broadcasted_iota(jnp.int32, (1, block), 1)
    lines = [item[rows : rows + 1, :].astype(jnp.float32).astype(jnp.int32) for item in items]
    for j in range(rows // block):
        left, right = [], []
        for s in range(len(items)):
            col = jnp.sum(jnp.where(lanes == part * (rows // block) + j, lines[s], 0))
            live = jnp.where(col < live_end, 1.0, 0.0).astype(jnp.float32)
            piece = items[s][j * block : (j + 1) * block, :]
            left.append((piece.astype(jnp.float32) * live).astype(jnp.bfloat16))
            at = pl.multiple_of(jnp.minimum(col, live_end - 1) * block, block)
            right.append(window[pl.ds(at, block), :])
        finish(
            j,
            jnp.dot(
                jnp.concatenate(left, axis=1),
                jnp.concatenate(right, axis=0),
                preferred_element_type=jnp.float32,
            ),
        )


def send_kernel(slots, *refs):
    items, (window, code_ref, total) = refs[:slots], refs[slots:]
    block = items[0].shape[1]
    rows = total.shape[0]

    def finish(j, value):
        total[j * block : (j + 1) * block, :] = value

    products(1 - lax.axis_index("layer"), items, window, finish)
    most = jnp.max(jnp.abs(total[...]), axis=0, keepdims=True)
    scale = (most * 1.01 + 1e-30).astype(jnp.bfloat16)
    inverse = CODE_SPAN / scale.astype(jnp.float32)
    for j in range(rows // block):
        value = total[j * block : (j + 1) * block, :]
        size = jnp.exp((jnp.abs(value) * inverse - CODE_MID) * (1.0 / LOG2E))
        code_ref[j * block : (j + 1) * block, :] = jnp.where(value < 0, -size, size).astype(jnp.bfloat16)
    code_ref[rows : rows + ID_ROWS, :] = jnp.broadcast_to(scale, (ID_ROWS, scale.shape[1]))


def keep_kernel(slots, *refs):
    items, (window, code_ref, square_ref, sum_ref) = refs[:slots], refs[slots:]
    block = items[0].shape[1]
    rows = square_ref.shape[0]
    scale = code_ref[rows : rows + 1, :].astype(jnp.float32) * (1.0 / CODE_SPAN)
    sums = []

    def finish(j, value):
        code = code_ref[j * block : (j + 1) * block, :].astype(jnp.float32)
        size = (jnp.log(jnp.abs(code)) * LOG2E + CODE_MID) * scale
        full = value + jnp.where(code < 0, -size, size)
        square = full * full
        square_ref[j * block : (j + 1) * block, :] = square
        sums.append(jnp.sum(square, axis=0, keepdims=True))

    products(lax.axis_index("layer"), items, window, finish)
    sum_ref[...] = functools.reduce(jnp.add, sums)


def solution(mesh):
    size = mesh.shape["col"]
    ring = [6, 4, 2, 0, 1, 3, 5, 7]
    across = [(ring[a], ring[b]) for a, b in ((6, 1), (5, 2), (2, 5), (1, 6), (3, 0), (0, 3), (7, 4), (4, 7))]

    def shift(hops):
        return [(ring[i], ring[(i + hops) % len(ring)]) for i in range(len(ring))]

    swap = [(0, 1), (1, 0)]
    vmem = pl.BlockSpec(memory_space=pltpu.VMEM)
    anywhere = pl.BlockSpec(memory_space=pl.ANY)

    def gather_all(item):
        stacked = lax.all_gather(item, "col", axis=0)
        return [stacked[i] for i in range(size)]

    def body(flow_cols, flow_vals, window_flow):
        block = flow_vals.shape[-1]
        count = flow_vals.shape[0] // 2
        rows = count * block
        own = window_flow[0]
        half, columns = own.shape
        item = jax.ShapeDtypeStruct((rows + ID_ROWS, block), flow_vals.dtype)
        params = pltpu.CompilerParams(vmem_limit_bytes=VMEM_BYTES)
        items = pl.pallas_call(
            pack_kernel,
            out_shape=(item,) * 2,
            in_specs=[vmem, anywhere],
            out_specs=(vmem,) * 2,
            scratch_shapes=[pltpu.SemaphoreType.DMA((2,))],
            compiler_params=params,
        )(flow_cols.reshape(1, 2 * count), flow_vals.reshape(2 * rows, block))
        theirs = own
        send, keep = items[:1] * 3, items[1:] * 3

        def pick(first, last):
            return pl.pallas_call(
                pick_kernel, out_shape=item, in_specs=[vmem, vmem], out_specs=vmem, compiler_params=params
            )(first, last)

        def place(mine, part, window=None):
            given = [] if window is None else [window]
            return pl.pallas_call(
                functools.partial(place_kernel, mine),
                out_shape=jax.ShapeDtypeStruct((2 * half, columns), own.dtype),
                in_specs=[anywhere] + [vmem] * len(given),
                out_specs=vmem,
                scratch_shapes=[pltpu.SemaphoreType.DMA(())],
                input_output_aliases={1: 0} if given else {},
                compiler_params=params,
                cost_estimate=pl.CostEstimate(flops=0, bytes_accessed=2 * half * columns * 2, transcendentals=0),
            )(part, *given)

        item_specs = [vmem] * size

        def coded(sends, window):
            return pl.pallas_call(
                functools.partial(send_kernel, size),
                out_shape=jax.ShapeDtypeStruct((rows + ID_ROWS, columns), jnp.bfloat16),
                in_specs=item_specs + [vmem],
                out_specs=vmem,
                scratch_shapes=[pltpu.VMEM((rows, columns), jnp.float32)],
                compiler_params=params,
            )(*sends, window)

        window = place(True, own)
        if size == 8:
            chosen = {}
            ends = {"S": (send[0], send[0]), "K": (keep[0], keep[0])}
            lists = {"S": [send[0]], "K": [keep[0]]}
            code = other = None

            def tie(names):
                nonlocal window, code, theirs, other
                given = {"W": window, "C": code, "T": theirs, "O": other}
                for n in "SK":
                    given[n] = (ends[n], lists[n][-1])
                    given[n + "p"] = chosen.get(n)
                done = lax.optimization_barrier(tuple(given[n] for n in names))
                for n, value in zip(names, done):
                    if n == "W":
                        window = value
                    elif n == "C":
                        code = value
                    elif n[-1] == "p":
                        chosen[n[0]] = value
                    elif n == "T":
                        theirs = value
                    elif n == "O":
                        other = value
                    else:
                        ends[n], lists[n][-1] = value

            for name in PLAN:
                if name == "O":
                    other = lax.ppermute(theirs, "row", swap)
                elif name == "J":
                    window = place(False, other, window)
                elif name == "C":
                    code = coded(lists["S"], window)
                elif name == "X":
                    code = lax.ppermute(code, "layer", swap)
                elif "=" in name:
                    tie(name.split("="))
                elif name[1] == "p":
                    chosen[name[0]] = pick(*ends[name[0]])
                elif name[1] == "m":
                    lists[name[0]].append(lax.ppermute(chosen[name[0]], "col", across))
                else:
                    kind = name[0]
                    ends[kind] = tuple(lax.ppermute(e, "col", shift(w)) for e, w in zip(ends[kind], (1, -1)))
                    lists[kind].extend(ends[kind])
            keeps = lists["K"]
        else:
            sends, keeps = gather_all(send[0]), gather_all(keep[0])
            window = place(False, lax.ppermute(own, "row", swap), window)
            code = lax.ppermute(coded(sends, window), "layer", swap)
        square, sums = pl.pallas_call(
            functools.partial(keep_kernel, size),
            out_shape=(
                jax.ShapeDtypeStruct((rows, columns), jnp.float32),
                jax.ShapeDtypeStruct((1, columns), jnp.float32),
            ),
            in_specs=item_specs + [vmem, vmem],
            out_specs=(vmem, vmem),
            compiler_params=params,
        )(*keeps, window, code)
        cross = [(0, 3), (1, 2), (2, 1), (3, 0)]
        sums = sums + lax.ppermute(sums, "row", swap) + lax.ppermute(sums, "layer", swap) + lax.ppermute(sums, ("row", "layer"), cross)
        total_rows = rows * lax.axis_size("row") * lax.axis_size("layer")
        return square * (1.0 / (sums / total_rows + 1e-6))

    placed = (
        P("row", "layer", "col"),
        P("row", "layer", "col", None, None),
        P("layer", "row", "col"),
    )
    return jax.shard_map(body, mesh=mesh, in_specs=placed, out_specs=P(("row", "layer"), "col"), check_vma=False)
```

```python
import functools

import jax
import jax.numpy as jnp
from jax import lax
from jax.experimental import pallas as pl
from jax.experimental.pallas import tpu as pltpu
from jax.sharding import PartitionSpec as P

CODE_SPAN = 250.0
CODE_MID = 125.0
LOG2E = 1.4426950408889634
ID_ROWS = 16
LATE = 3
VMEM_BYTES = 24 * 1024 * 1024
PLAN = ("S=K=T", "O", "S1", "K1", "S=W", "Sp", "Kp", "S2", "K2", "J", "S=W=Sp=Kp", "S3", "Sm", "S=K", "C", "X", "K3", "Km")


def pack_kernel(cols_ref, vals_ref, *refs):
    outs, sems = refs[:-1], refs[-1]
    rows = outs[0].shape[0] - ID_ROWS
    block = vals_ref.shape[1]
    layer = lax.axis_index("layer")
    copies = []
    for k, out in enumerate(outs):
        part = 1 - layer if k < len(outs) // 2 else layer
        copies.append(
            pltpu.make_async_copy(
                vals_ref.at[pl.ds(pl.multiple_of(part * rows, block), rows)],
                out.at[pl.ds(0, rows)],
                sems.at[k],
            )
        )
        copies[-1].start()
    line = jnp.pad(cols_ref[...], ((0, 0), (0, block - cols_ref.shape[1])))
    line = jnp.broadcast_to(line, (ID_ROWS, block)).astype(jnp.float32).astype(jnp.bfloat16)
    for out in outs:
        out[rows : rows + ID_ROWS, :] = line
    for copy in copies:
        copy.wait()


def pick_kernel(first_ref, last_ref, out_ref):
    col = lax.axis_index("col")
    odd = lax.rem(col + lax.div(col, 2) + 1, 2)

    @pl.when(odd == 0)
    def _():
        out_ref[...] = first_ref[...]

    @pl.when(odd != 0)
    def _():
        out_ref[...] = last_ref[...]


def place_kernel(mine, part_ref, *refs):
    window_ref, sem = refs[-2:]
    half = part_ref.shape[0]
    row = lax.axis_index("row")
    where = pl.ds(pl.multiple_of((row if mine else 1 - row) * half, half), half)
    copy = pltpu.make_async_copy(part_ref, window_ref.at[where], sem)
    copy.start()
    copy.wait()


def products(part, items, window, finish):
    block = items[0].shape[1]
    rows = items[0].shape[0] - ID_ROWS
    live_end = window.shape[0] // block
    lanes = lax.broadcasted_iota(jnp.int32, (1, block), 1)
    lines = [item[rows : rows + 1, :].astype(jnp.float32).astype(jnp.int32) for item in items]
    for j in range(rows // block):
        left, right = [], []
        for s in range(len(items)):
            col = jnp.sum(jnp.where(lanes == part * (rows // block) + j, lines[s], 0))
            live = jnp.where(col < live_end, 1.0, 0.0).astype(jnp.float32)
            piece = items[s][j * block : (j + 1) * block, :]
            left.append((piece.astype(jnp.float32) * live).astype(jnp.bfloat16))
            at = pl.multiple_of(jnp.minimum(col, live_end - 1) * block, block)
            right.append(window[pl.ds(at, block), :])
        finish(
            j,
            jnp.dot(
                jnp.concatenate(left, axis=1),
                jnp.concatenate(right, axis=0),
                preferred_element_type=jnp.float32,
            ),
        )


def early_kernel(slots, kept, *refs):
    items, (window, total) = refs[:slots], refs[slots:]
    block = items[0].shape[1]
    layer = lax.axis_index("layer")

    def finish(j, value):
        total[j * block : (j + 1) * block, :] = value

    products(layer if kept else 1 - layer, items, window, finish)


def send_kernel(slots, *refs):
    items, (window, early, code_ref, total) = refs[:slots], refs[slots:]
    block = items[0].shape[1]
    rows = total.shape[0]

    def finish(j, value):
        total[j * block : (j + 1) * block, :] = value + early[j * block : (j + 1) * block, :]

    products(1 - lax.axis_index("layer"), items, window, finish)
    most = jnp.max(jnp.abs(total[...]), axis=0, keepdims=True)
    scale = (most * 1.01 + 1e-30).astype(jnp.bfloat16)
    inverse = CODE_SPAN / scale.astype(jnp.float32)
    for j in range(rows // block):
        value = total[j * block : (j + 1) * block, :]
        size = jnp.exp((jnp.abs(value) * inverse - CODE_MID) * (1.0 / LOG2E))
        code_ref[j * block : (j + 1) * block, :] = jnp.where(value < 0, -size, size).astype(jnp.bfloat16)
    code_ref[rows : rows + ID_ROWS, :] = jnp.broadcast_to(scale, (ID_ROWS, scale.shape[1]))


def keep_kernel(slots, *refs):
    items, (window, code_ref, square_ref, sum_ref) = refs[:slots], refs[slots:]
    block = items[0].shape[1]
    rows = square_ref.shape[0]
    scale = code_ref[rows : rows + 1, :].astype(jnp.float32) * (1.0 / CODE_SPAN)
    sums = []

    def finish(j, value):
        code = code_ref[j * block : (j + 1) * block, :].astype(jnp.float32)
        size = (jnp.log(jnp.abs(code)) * LOG2E + CODE_MID) * scale
        full = value + jnp.where(code < 0, -size, size)
        square = full * full
        square_ref[j * block : (j + 1) * block, :] = square
        sums.append(jnp.sum(square, axis=0, keepdims=True))

    products(lax.axis_index("layer"), items, window, finish)
    sum_ref[...] = functools.reduce(jnp.add, sums)


def solution(mesh):
    size = mesh.shape["col"]
    ring = [6, 4, 2, 0, 1, 3, 5, 7]
    across = [(ring[a], ring[b]) for a, b in ((6, 1), (5, 2), (2, 5), (1, 6), (3, 0), (0, 3), (7, 4), (4, 7))]

    def shift(hops):
        return [(ring[i], ring[(i + hops) % len(ring)]) for i in range(len(ring))]

    swap = [(0, 1), (1, 0)]
    vmem = pl.BlockSpec(memory_space=pltpu.VMEM)
    anywhere = pl.BlockSpec(memory_space=pl.ANY)

    def gather_all(item):
        stacked = lax.all_gather(item, "col", axis=0)
        return [stacked[i] for i in range(size)]

    def body(flow_cols, flow_vals, window_flow):
        block = flow_vals.shape[-1]
        count = flow_vals.shape[0] // 2
        rows = count * block
        own = window_flow[0]
        half, columns = own.shape
        item = jax.ShapeDtypeStruct((rows + ID_ROWS, block), flow_vals.dtype)
        params = pltpu.CompilerParams(vmem_limit_bytes=VMEM_BYTES)
        items = pl.pallas_call(
            pack_kernel,
            out_shape=(item,) * 2,
            in_specs=[vmem, anywhere],
            out_specs=(vmem,) * 2,
            scratch_shapes=[pltpu.SemaphoreType.DMA((2,))],
            compiler_params=params,
        )(flow_cols.reshape(1, 2 * count), flow_vals.reshape(2 * rows, block))
        theirs = own
        send, keep = items[:1] * 3, items[1:] * 3

        def pick(first, last):
            return pl.pallas_call(
                pick_kernel, out_shape=item, in_specs=[vmem, vmem], out_specs=vmem, compiler_params=params
            )(first, last)

        def place(mine, part, window=None):
            given = [] if window is None else [window]
            return pl.pallas_call(
                functools.partial(place_kernel, mine),
                out_shape=jax.ShapeDtypeStruct((2 * half, columns), own.dtype),
                in_specs=[anywhere] + [vmem] * len(given),
                out_specs=vmem,
                scratch_shapes=[pltpu.SemaphoreType.DMA(())],
                input_output_aliases={1: 0} if given else {},
                compiler_params=params,
                cost_estimate=pl.CostEstimate(flops=0, bytes_accessed=2 * half * columns * 2, transcendentals=0),
            )(part, *given)

        def started(items, window, kept):
            return pl.pallas_call(
                functools.partial(early_kernel, len(items), kept),
                out_shape=jax.ShapeDtypeStruct((rows, columns), jnp.float32),
                in_specs=[vmem] * (len(items) + 1),
                out_specs=vmem,
                compiler_params=params,
            )(*items, window)


        def coded(sends, window):
            return pl.pallas_call(
                functools.partial(send_kernel, LATE),
                out_shape=jax.ShapeDtypeStruct((rows + ID_ROWS, columns), jnp.bfloat16),
                in_specs=[vmem] * (LATE + 2),
                out_specs=vmem,
                scratch_shapes=[pltpu.VMEM((rows, columns), jnp.float32)],
                compiler_params=params,
            )(*sends[-LATE:], window, started(sends[:-LATE], window, False))

        window = place(True, own)
        if size == 8:
            chosen = {}
            ends = {"S": (send[0], send[0]), "K": (keep[0], keep[0])}
            lists = {"S": [send[0]], "K": [keep[0]]}
            code = other = None

            def tie(names):
                nonlocal window, code, theirs, other
                given = {"W": window, "C": code, "T": theirs, "O": other}
                for n in "SK":
                    given[n] = (ends[n], lists[n][-1])
                    given[n + "p"] = chosen.get(n)
                done = lax.optimization_barrier(tuple(given[n] for n in names))
                for n, value in zip(names, done):
                    if n == "W":
                        window = value
                    elif n == "C":
                        code = value
                    elif n[-1] == "p":
                        chosen[n[0]] = value
                    elif n == "T":
                        theirs = value
                    elif n == "O":
                        other = value
                    else:
                        ends[n], lists[n][-1] = value

            for name in PLAN:
                if name == "O":
                    other = lax.ppermute(theirs, "row", swap)
                elif name == "J":
                    window = place(False, other, window)
                elif name == "C":
                    code = coded(lists["S"], window)
                elif name == "X":
                    code = lax.ppermute(code, "layer", swap)
                elif "=" in name:
                    tie(name.split("="))
                elif name[1] == "p":
                    chosen[name[0]] = pick(*ends[name[0]])
                elif name[1] == "m":
                    lists[name[0]].append(lax.ppermute(chosen[name[0]], "col", across))
                else:
                    kind = name[0]
                    ends[kind] = tuple(lax.ppermute(e, "col", shift(w)) for e, w in zip(ends[kind], (1, -1)))
                    lists[kind].extend(ends[kind])
            keeps = lists["K"]
        else:
            sends, keeps = gather_all(send[0]), gather_all(keep[0])
            window = place(False, lax.ppermute(own, "row", swap), window)
            code = lax.ppermute(coded(sends, window), "layer", swap)
        square, sums = pl.pallas_call(
            functools.partial(keep_kernel, size),
            out_shape=(
                jax.ShapeDtypeStruct((rows, columns), jnp.float32),
                jax.ShapeDtypeStruct((1, columns), jnp.float32),
            ),
            in_specs=[vmem] * (size + 2),
            out_specs=(vmem, vmem),
            compiler_params=params,
        )(*keeps, window, code)
        cross = [(0, 3), (1, 2), (2, 1), (3, 0)]
        sums = sums + lax.ppermute(sums, "row", swap) + lax.ppermute(sums, "layer", swap) + lax.ppermute(sums, ("row", "layer"), cross)
        total_rows = rows * lax.axis_size("row") * lax.axis_size("layer")
        return square * (1.0 / (sums / total_rows + 1e-6))

    placed = (
        P("row", "layer", "col"),
        P("row", "layer", "col", None, None),
        P("layer", "row", "col"),
    )
    return jax.shard_map(body, mesh=mesh, in_specs=placed, out_specs=P(("row", "layer"), "col"), check_vma=False)
```

```python
import functools

import jax
import jax.numpy as jnp
from jax import lax
from jax.experimental import pallas as pl
from jax.experimental.pallas import tpu as pltpu
from jax.sharding import PartitionSpec as P

CODE_SPAN = 250.0
CODE_MID = 125.0
LOG2E = 1.4426950408889634
ID_ROWS = 16
LATE = 3
VMEM_BYTES = 24 * 1024 * 1024
PLAN = ("S=K=T", "O", "S1", "K1", "S=W", "Sp", "Kp", "S2", "K2", "J", "S=W=Sp=Kp", "S3", "Sm", "S=K", "C", "X", "Km", "K3")


def pack_kernel(cols_ref, vals_ref, *refs):
    outs, sems = refs[:-1], refs[-1]
    rows = outs[0].shape[0] - ID_ROWS
    block = vals_ref.shape[1]
    layer = lax.axis_index("layer")
    copies = []
    for k, out in enumerate(outs):
        part = 1 - layer if k < len(outs) // 2 else layer
        copies.append(
            pltpu.make_async_copy(
                vals_ref.at[pl.ds(pl.multiple_of(part * rows, block), rows)],
                out.at[pl.ds(0, rows)],
                sems.at[k],
            )
        )
        copies[-1].start()
    line = jnp.pad(cols_ref[...], ((0, 0), (0, block - cols_ref.shape[1])))
    line = jnp.broadcast_to(line, (ID_ROWS, block)).astype(jnp.float32).astype(jnp.bfloat16)
    for out in outs:
        out[rows : rows + ID_ROWS, :] = line
    for copy in copies:
        copy.wait()


def pick_kernel(first_ref, last_ref, out_ref):
    col = lax.axis_index("col")
    odd = lax.rem(col + lax.div(col, 2) + 1, 2)

    @pl.when(odd == 0)
    def _():
        out_ref[...] = first_ref[...]

    @pl.when(odd != 0)
    def _():
        out_ref[...] = last_ref[...]


def place_kernel(mine, part_ref, *refs):
    window_ref, sem = refs[-2:]
    half = part_ref.shape[0]
    row = lax.axis_index("row")
    where = pl.ds(pl.multiple_of((row if mine else 1 - row) * half, half), half)
    copy = pltpu.make_async_copy(part_ref, window_ref.at[where], sem)
    copy.start()
    copy.wait()


def products(part, items, window, finish):
    block = items[0].shape[1]
    rows = items[0].shape[0] - ID_ROWS
    live_end = window.shape[0] // block
    lanes = lax.broadcasted_iota(jnp.int32, (1, block), 1)
    lines = [item[rows : rows + 1, :].astype(jnp.float32).astype(jnp.int32) for item in items]
    for j in range(rows // block):
        left, right = [], []
        for s in range(len(items)):
            col = jnp.sum(jnp.where(lanes == part * (rows // block) + j, lines[s], 0))
            live = jnp.where(col < live_end, 1.0, 0.0).astype(jnp.float32)
            piece = items[s][j * block : (j + 1) * block, :]
            left.append((piece.astype(jnp.float32) * live).astype(jnp.bfloat16))
            at = pl.multiple_of(jnp.minimum(col, live_end - 1) * block, block)
            right.append(window[pl.ds(at, block), :])
        finish(
            j,
            jnp.dot(
                jnp.concatenate(left, axis=1),
                jnp.concatenate(right, axis=0),
                preferred_element_type=jnp.float32,
            ),
        )


def early_kernel(slots, kept, *refs):
    items, (window, total) = refs[:slots], refs[slots:]
    block = items[0].shape[1]
    layer = lax.axis_index("layer")

    def finish(j, value):
        total[j * block : (j + 1) * block, :] = value

    products(layer if kept else 1 - layer, items, window, finish)


def send_kernel(slots, *refs):
    items, (window, early, code_ref, total) = refs[:slots], refs[slots:]
    block = items[0].shape[1]
    rows = total.shape[0]

    def finish(j, value):
        total[j * block : (j + 1) * block, :] = value + early[j * block : (j + 1) * block, :]

    products(1 - lax.axis_index("layer"), items, window, finish)
    most = jnp.max(jnp.abs(total[...]), axis=0, keepdims=True)
    scale = (most * 1.01 + 1e-30).astype(jnp.bfloat16)
    inverse = CODE_SPAN / scale.astype(jnp.float32)
    for j in range(rows // block):
        value = total[j * block : (j + 1) * block, :]
        size = jnp.exp((jnp.abs(value) * inverse - CODE_MID) * (1.0 / LOG2E))
        code_ref[j * block : (j + 1) * block, :] = jnp.where(value < 0, -size, size).astype(jnp.bfloat16)
    code_ref[rows : rows + ID_ROWS, :] = jnp.broadcast_to(scale, (ID_ROWS, scale.shape[1]))


def keep_kernel(slots, *refs):
    items, (window, early, code_ref, square_ref, sum_ref) = refs[:slots], refs[slots:]
    block = items[0].shape[1]
    rows = square_ref.shape[0]
    scale = code_ref[rows : rows + 1, :].astype(jnp.float32) * (1.0 / CODE_SPAN)
    sums = []

    def finish(j, value):
        code = code_ref[j * block : (j + 1) * block, :].astype(jnp.float32)
        size = (jnp.log(jnp.abs(code)) * LOG2E + CODE_MID) * scale
        full = value + early[j * block : (j + 1) * block, :] + jnp.where(code < 0, -size, size)
        square = full * full
        square_ref[j * block : (j + 1) * block, :] = square
        sums.append(jnp.sum(square, axis=0, keepdims=True))

    products(lax.axis_index("layer"), items, window, finish)
    sum_ref[...] = functools.reduce(jnp.add, sums)


def solution(mesh):
    size = mesh.shape["col"]
    ring = [6, 4, 2, 0, 1, 3, 5, 7]
    across = [(ring[a], ring[b]) for a, b in ((6, 1), (5, 2), (2, 5), (1, 6), (3, 0), (0, 3), (7, 4), (4, 7))]

    def shift(hops):
        return [(ring[i], ring[(i + hops) % len(ring)]) for i in range(len(ring))]

    swap = [(0, 1), (1, 0)]
    vmem = pl.BlockSpec(memory_space=pltpu.VMEM)
    anywhere = pl.BlockSpec(memory_space=pl.ANY)

    def gather_all(item):
        stacked = lax.all_gather(item, "col", axis=0)
        return [stacked[i] for i in range(size)]

    def body(flow_cols, flow_vals, window_flow):
        block = flow_vals.shape[-1]
        count = flow_vals.shape[0] // 2
        rows = count * block
        own = window_flow[0]
        half, columns = own.shape
        item = jax.ShapeDtypeStruct((rows + ID_ROWS, block), flow_vals.dtype)
        params = pltpu.CompilerParams(vmem_limit_bytes=VMEM_BYTES)
        items = pl.pallas_call(
            pack_kernel,
            out_shape=(item,) * 2,
            in_specs=[vmem, anywhere],
            out_specs=(vmem,) * 2,
            scratch_shapes=[pltpu.SemaphoreType.DMA((2,))],
            compiler_params=params,
        )(flow_cols.reshape(1, 2 * count), flow_vals.reshape(2 * rows, block))
        theirs = own
        send, keep = items[:1] * 3, items[1:] * 3

        def pick(first, last):
            return pl.pallas_call(
                pick_kernel, out_shape=item, in_specs=[vmem, vmem], out_specs=vmem, compiler_params=params
            )(first, last)

        def place(mine, part, window=None):
            given = [] if window is None else [window]
            return pl.pallas_call(
                functools.partial(place_kernel, mine),
                out_shape=jax.ShapeDtypeStruct((2 * half, columns), own.dtype),
                in_specs=[anywhere] + [vmem] * len(given),
                out_specs=vmem,
                scratch_shapes=[pltpu.SemaphoreType.DMA(())],
                input_output_aliases={1: 0} if given else {},
                compiler_params=params,
                cost_estimate=pl.CostEstimate(flops=0, bytes_accessed=2 * half * columns * 2, transcendentals=0),
            )(part, *given)

        def started(items, window, kept):
            return pl.pallas_call(
                functools.partial(early_kernel, len(items), kept),
                out_shape=jax.ShapeDtypeStruct((rows, columns), jnp.float32),
                in_specs=[vmem] * (len(items) + 1),
                out_specs=vmem,
                compiler_params=params,
            )(*items, window)


        def coded(sends, window):
            return pl.pallas_call(
                functools.partial(send_kernel, LATE),
                out_shape=jax.ShapeDtypeStruct((rows + ID_ROWS, columns), jnp.bfloat16),
                in_specs=[vmem] * (LATE + 2),
                out_specs=vmem,
                scratch_shapes=[pltpu.VMEM((rows, columns), jnp.float32)],
                compiler_params=params,
            )(*sends[-LATE:], window, started(sends[:-LATE], window, False))

        window = place(True, own)
        if size == 8:
            chosen = {}
            ends = {"S": (send[0], send[0]), "K": (keep[0], keep[0])}
            lists = {"S": [send[0]], "K": [keep[0]]}
            code = other = None

            def tie(names):
                nonlocal window, code, theirs, other
                given = {"W": window, "C": code, "T": theirs, "O": other}
                for n in "SK":
                    given[n] = (ends[n], lists[n][-1])
                    given[n + "p"] = chosen.get(n)
                done = lax.optimization_barrier(tuple(given[n] for n in names))
                for n, value in zip(names, done):
                    if n == "W":
                        window = value
                    elif n == "C":
                        code = value
                    elif n[-1] == "p":
                        chosen[n[0]] = value
                    elif n == "T":
                        theirs = value
                    elif n == "O":
                        other = value
                    else:
                        ends[n], lists[n][-1] = value

            for name in PLAN:
                if name == "O":
                    other = lax.ppermute(theirs, "row", swap)
                elif name == "J":
                    window = place(False, other, window)
                elif name == "C":
                    code = coded(lists["S"], window)
                elif name == "X":
                    code = lax.ppermute(code, "layer", swap)
                elif "=" in name:
                    tie(name.split("="))
                elif name[1] == "p":
                    chosen[name[0]] = pick(*ends[name[0]])
                elif name[1] == "m":
                    lists[name[0]].append(lax.ppermute(chosen[name[0]], "col", across))
                else:
                    kind = name[0]
                    ends[kind] = tuple(lax.ppermute(e, "col", shift(w)) for e, w in zip(ends[kind], (1, -1)))
                    lists[kind].extend(ends[kind])
            keeps = lists["K"]
        else:
            sends, keeps = gather_all(send[0]), gather_all(keep[0])
            window = place(False, lax.ppermute(own, "row", swap), window)
            code = lax.ppermute(coded(sends, window), "layer", swap)
        square, sums = pl.pallas_call(
            functools.partial(keep_kernel, LATE),
            out_shape=(
                jax.ShapeDtypeStruct((rows, columns), jnp.float32),
                jax.ShapeDtypeStruct((1, columns), jnp.float32),
            ),
            in_specs=[vmem] * (LATE + 3),
            out_specs=(vmem, vmem),
            compiler_params=params,
        )(*keeps[-LATE:], window, started(keeps[:-LATE], window, True), code)
        cross = [(0, 3), (1, 2), (2, 1), (3, 0)]
        sums = sums + lax.ppermute(sums, "row", swap) + lax.ppermute(sums, "layer", swap) + lax.ppermute(sums, ("row", "layer"), cross)
        total_rows = rows * lax.axis_size("row") * lax.axis_size("layer")
        return square * (1.0 / (sums / total_rows + 1e-6))

    placed = (
        P("row", "layer", "col"),
        P("row", "layer", "col", None, None),
        P("layer", "row", "col"),
    )
    return jax.shard_map(body, mesh=mesh, in_specs=placed, out_specs=P(("row", "layer"), "col"), check_vma=False)
```
